128 devices in a mesh: mult: 4 (over z_lo, core), chan: 32 (over z_hi, x, y).
Axes of the slice: x: 4, y: 4, z: 4 (z_hi: 2, z_lo: 2; z = z_hi * 2 + z_lo), core: 2. Of those that a mesh axis runs over, the one named last changes fastest.
Arguments:
- columns: float32 [256, 1024, 128], P('chan'), may hold values from -6 to 6
- panels: float32 [8, 2, 1024, 1024], P('mult', None, 'chan'), may hold values from -0.1875 to 0.1875
- coefficients: float32 [256, 16, 8], P('chan', None, 'mult'), may hold values from -2 to 2
- channel_cols: int32 [256, 16], P('chan'), may hold values from 0 to 255, as said below
- used_slots: int32 [256], P('chan'), may hold values from 1 to 16, as said below
- lambda_low: int32 [256, 16], P('chan'), may hold values from 0 to 3
- lambda_high: int32 [256, 16], P('chan'), may hold values from 5 to 8
- energies: float32 [256], P('chan'), may hold values from 0 to 2
- contour: float32 [2], replicated, may hold values from 0.5 to 1.5
Outputs:
- filtered: float32 [256, 1024, 128], P('chan', 'mult')
The draws below stay inside these ranges and needn't reach their ends.
Inputs may be any that keep to these rules, and one draw needn't show every extreme that they name: channel_cols[i, s] // 8 differs from i // 8 by at most 2, and channel_cols[i, 0] = i. `used_slots`: some channel uses all 16 slots.
All inputs are finite; a program needn't handle non-finite values.
Results may differ from the reference program's by a relative error of at most 0.0001.
Values sent between devices are 32-bit elements; how exact they have to be, the bound alone decides.
A program may use at most 192 MiB of HBM per device.

```python
import jax
import jax.numpy as jnp
from jax import lax

NB = 1024
K = 64
NL = 8
MAXNZ = 16
R = 2
CH_DEV = 8
NCH = 256


def draw_channel_cols(key, part):
    key_offset, key_inner = jax.random.split(key)
    row_ids = jnp.arange(NCH, dtype=jnp.int32)
    own_block = row_ids // CH_DEV
    offset = jax.random.randint(key_offset, (NCH, MAXNZ), -R, R + 1)
    in_block = jax.random.randint(key_inner, (NCH, MAXNZ), 0, CH_DEV)
    target = own_block[:, None] + offset
    inside = (target >= 0) & (target < NCH // CH_DEV)
    target = jnp.where(inside, target, own_block[:, None])
    picked = target * CH_DEV + in_block
    first_slot = jnp.arange(MAXNZ, dtype=jnp.int32)[None, :] == 0
    return jnp.where(first_slot, row_ids[:, None], picked).astype(jnp.int32)


def draw_used_slots(key, part):
    key_count, key_full = jax.random.split(key)
    counts = jax.random.randint(key_count, (NCH,), 1, MAXNZ + 1)
    fullest = jax.random.randint(key_full, (), 0, NCH)
    return jnp.where(jnp.arange(NCH, dtype=jnp.int32) == fullest, MAXNZ, counts).astype(jnp.int32)


def touch_ends(entries, rng, low, largest):
    shape = entries.shape
    index_at = [jax.random.randint(jax.random.fold_in(rng, axis), (), 0, shape[axis]) for axis in range(len(shape))]
    entries = entries.at[tuple(index_at)].set(low)
    longest = shape.index(max(shape))
    index_at[longest] = (index_at[longest] + 1) % shape[longest]
    return entries.at[tuple(index_at)].set(largest)


def level_of(own_key, extent, cuts, smallest, largest):
    gain, own = 1.0, jax.random.fold_in(own_key, 6)
    for dim, parts in cuts:
        heights = jnp.exp(jax.random.uniform(jax.random.fold_in(own, dim), (parts,), jnp.float32, smallest / len(cuts), largest / len(cuts)))
        gain = gain * jnp.repeat(heights, extent[dim] // parts).reshape([-1 if axis == dim else 1 for axis in range(len(extent))])
    return gain


def scatter_about(stream_key, extent, width, reach, cuts=(), kind=jnp.bfloat16):
    result = jax.random.normal(stream_key, extent, jnp.float32) * width
    if len(cuts) > 0:
        result = level_of(stream_key, extent, cuts, -0.22, 0.18) * result
    return jnp.clip(result, min=-reach, max=reach).astype(kind)


def setup_inputs(seed: int = 0) -> dict:
    seeds = jax.random.split(jax.random.key(seed), 10)
    columns = scatter_about(seeds[0], (NCH, NB, 2 * K), 1.0, 6.0, ((0, 32),), jnp.float32)
    panels = scatter_about(seeds[1], (NL, 2, NB, NB), NB ** -0.5, 0.1875, ((0, 4), (2, 32)), jnp.float32)
    coefficients = scatter_about(seeds[2], (NCH, MAXNZ, NL), 0.15, 2.0, ((0, 32), (2, 4)), jnp.float32)
    channel_cols = draw_channel_cols(jax.random.fold_in(seeds[9], 71), 0)
    used_slots = draw_used_slots(jax.random.fold_in(seeds[9], 71), 0)
    lambda_low = touch_ends(jax.random.randint(seeds[5], (NCH, MAXNZ), 0, NL // 2), jax.random.fold_in(seeds[5], 1), 0, (NL // 2) - 1).astype(jnp.int32)
    lambda_high = touch_ends(jax.random.randint(seeds[6], (NCH, MAXNZ), NL // 2 + 1, NL + 1), jax.random.fold_in(seeds[6], 1), NL // 2 + 1, NL).astype(jnp.int32)
    energies = jnp.clip(2.0 * jax.random.uniform(seeds[7], (NCH,), jnp.float32) ** level_of(seeds[7], (NCH,), ((0, 32),), -0.2, 0.2), 0.0, 2.0)
    contour = jnp.clip(jax.random.uniform(seeds[8], (2,), jnp.float32, 0.5, 1.5), 0.5, 1.5)
    return {"columns": columns, "panels": panels, "coefficients": coefficients, "channel_cols": channel_cols, "used_slots": used_slots, "lambda_low": lambda_low, "lambda_high": lambda_high, "energies": energies, "contour": contour}


def reference(columns, panels, coefficients, channel_cols, used_slots, lambda_low, lambda_high, energies, contour):
    half_width = columns.shape[2] // 2
    slot_ids = jnp.arange(MAXNZ, dtype=jnp.int32)
    live_slot = slot_ids[None, :] < used_slots[:, None]
    lambda_ids = jnp.arange(NL, dtype=jnp.int32)
    in_range = (lambda_ids[None, None, :] >= lambda_low[:, :, None]) & (lambda_ids[None, None, :] < lambda_high[:, :, None])
    weights = jnp.where(live_slot[:, :, None] & in_range, coefficients, jnp.zeros_like(coefficients))
    one_hot = (channel_cols[:, :, None] == jnp.arange(NCH, dtype=jnp.int32)[None, None, :]).astype(columns.dtype)
    mixing = jnp.einsum('isj,isl->ijl', one_hot, weights, precision=lax.Precision.HIGHEST)

    def per_order(total, order_id):
        panel = panels[order_id]
        real_prod = jnp.einsum('ab,cbk->cak', panel[0], columns, precision=lax.Precision.HIGHEST)
        imag_prod = jnp.einsum('ab,cbk->cak', panel[1], columns, precision=lax.Precision.HIGHEST)
        product = jnp.concatenate([real_prod[..., :half_width] - imag_prod[..., half_width:], real_prod[..., half_width:] + imag_prod[..., :half_width]], axis=-1)
        mix_now = mixing[:, :, order_id]
        return total + jnp.einsum('ij,jak->iak', mix_now, product, precision=lax.Precision.HIGHEST), None

    coupled, _ = lax.scan(per_order, jnp.zeros_like(columns), jnp.arange(NL, dtype=jnp.int32))
    energy_shift = (contour[0] - energies)[:, None, None]
    imag_shift = contour[1]
    real_part = columns[..., :half_width]
    imag_part = columns[..., half_width:]
    out_real = energy_shift * real_part - imag_shift * imag_part - coupled[..., :half_width]
    out_imag = energy_shift * imag_part + imag_shift * real_part - coupled[..., half_width:]
    return jnp.concatenate([out_real, out_imag], axis=-1)
```

```python
import jax
import jax.numpy as jnp
from jax import lax
from jax.experimental import pallas as pl
from jax.experimental.pallas import tpu as pltpu
from jax.sharding import PartitionSpec as P

MAXNZ = 16
MESH = pl.DeviceIdType.MESH
F32 = jnp.float32
BF16 = jnp.bfloat16
NB = 1024


def place():
    mi = lax.axis_index("mult")
    ci = lax.axis_index("chan")
    return mi // 2, mi % 2, ci // 16, (ci // 4) % 4, ci % 4


def device(z_lo, core, z_hi, x, y):
    return (z_lo * 2 + core, z_hi * 16 + x * 4 + y)


def split(value):
    high = value.astype(BF16)
    return high, (value - high.astype(F32)).astype(BF16)


def swap_halves(value):
    lane = lax.broadcasted_iota(jnp.int32, value.shape, value.ndim - 1)
    rolled = pltpu.roll(value, 64, value.ndim - 1)
    return jnp.where(lane < 64, -rolled, rolled)


def product_kernel(
    columns, panels, z_out,
    raw, p_high, p_low, blocks, z_buf, x_high, x_low,
    own_sem, first_send, p_send, p_recv, x_send, x_recv, s_send, s_recv, z_sem,
):
    z_lo, core, z_hi, x, y = place()
    left_x, right_x = (x + 3) % 4, (x + 1) % 4
    left_y, right_y = (y + 3) % 4, (y + 1) % 4
    to_left_x = device(z_lo, core, z_hi, left_x, y)
    to_right_x = device(z_lo, core, z_hi, right_x, y)
    to_left_y = device(z_lo, core, z_hi, x, left_y)
    to_right_y = device(z_lo, core, z_hi, x, right_y)
    sibling = device(z_lo, 1 - core, z_hi, x, y)
    target_x = (x + 2 * core + 3) % 4
    targets = [device(z_hi, x // 2, zh, target_x, y) for zh in range(2)]

    def origin(at_x):
        row_part = 1 - at_x % 2
        from_x = 2 * core + row_part
        from_core = jnp.where((from_x + 1) % 4 == at_x, 1, 0)
        return row_part, from_x, from_core

    row_part0, from_x0, from_core0 = origin(x)
    sources = [device(zl, from_core0, z_lo, from_x0, y) for zl in range(2)]
    spots = [origin(at) for at in (x, left_x, right_x, (x + 2) % 4)]

    barrier = pltpu.get_barrier_semaphore()
    peers = [to_left_x, to_right_x, to_left_y, to_right_y, sibling] + targets + sources
    for peer in peers:
        pl.semaphore_signal(barrier, inc=1, device_id=peer, device_id_type=MESH)
    pl.semaphore_wait(barrier, len(peers))

    def remote(src, dst, send_sem, recv_sem, peer):
        return pltpu.make_async_remote_copy(
            src_ref=src, dst_ref=dst, send_sem=send_sem, recv_sem=recv_sem,
            device_id=peer, device_id_type=MESH,
        )

    def piece(q):
        return pl.ds(4 * core + 2 * q, 2)

    def other_piece(q):
        return pl.ds(4 * (1 - core) + 2 * q, 2)

    sent = []

    def start(copy):
        copy.start()
        sent.append(copy)

    for k in range(2):
        start(remote(panels, raw.at[0, z_lo], first_send.at[k], p_recv.at[0, z_lo], targets[k]))
    for k, (q_right, q_left) in enumerate(((0, 1), (1, 0))):
        start(remote(columns.at[piece(q_right)], blocks.at[1, piece(q_right)],
                     x_send.at[0, q_right], x_recv.at[1, q_right], to_right_y))
        start(remote(columns.at[piece(q_left)], blocks.at[2, piece(q_left)],
                     x_send.at[1, q_left], x_recv.at[2, q_left], to_left_y))
    own = pltpu.make_async_copy(columns, blocks.at[0], own_sem)
    own.start()

    def wait_p(slot, zl):
        remote(raw.at[slot, zl], raw.at[slot, zl], p_send.at[0, zl], p_recv.at[slot, zl], to_right_x).wait_recv()

    def wait_x(block, q):
        ref = blocks.at[block, piece(q)]
        remote(ref, ref, x_send.at[0, q], x_recv.at[block, q], to_right_y).wait_recv()

    def to_sibling(block, q):
        ref = blocks.at[block, piece(q)]
        start(remote(ref, ref, s_send.at[block, q], s_recv.at[block, q], sibling))

    def wait_sibling(block, q):
        ref = blocks.at[block, other_piece(q)]
        remote(ref, ref, s_send.at[block, q], s_recv.at[block, q], sibling).wait_recv()

    def convert(slot):
        row_part, _, from_core = spots[slot]
        for zl in range(2):
            for order in range(2):
                at = row_part * 8 + 4 * zl + 2 * from_core + order
                for ri in range(2):
                    high, low = split(raw[slot, zl, order, ri])
                    p_high[at, ri] = high
                    p_low[at, ri] = low

    def load_piece(block, first):
        both = jnp.concatenate([blocks[block, first], blocks[block, first + 1]], axis=1)
        high, low = split(both)
        x_high[...] = high
        x_low[...] = low

    def multiply(ph, plo):
        high = x_high[...]
        acc = jnp.dot(ph, high, preferred_element_type=F32)
        acc += jnp.dot(plo, high, preferred_element_type=F32)
        acc += jnp.dot(ph, x_low[...], preferred_element_type=F32)
        return acc

    def store(acc, count, at, channel):
        acc = acc.reshape(count, 2, 32, 256)
        for half in range(2):
            part = acc[..., half * 128:half * 128 + 128]
            z_buf[channel + half, pl.ds(at, count)] = part[:, 0] + swap_halves(part[:, 1])

    def own_times(slot):
        row_part, _, from_core = spots[slot]

        def body(k, carry):
            load_piece(0, 2 * k)
            ats = [row_part * 8 + 4 * zl + 2 * from_core for zl in range(2)]
            ph = jnp.concatenate([p_high[pl.ds(at, 2)] for at in ats], axis=0).reshape(256, NB)
            plo = jnp.concatenate([p_low[pl.ds(at, 2)] for at in ats], axis=0).reshape(256, NB)
            acc = multiply(ph, plo)
            for zl in range(2):
                store(acc[zl * 128:zl * 128 + 128], 2, ats[zl], y * 8 + 2 * k)
            return carry

        lax.fori_loop(0, 4, body, 0)

    def piece_times(block, at_y, firsts):
        def body(k, carry):
            first = firsts(k)
            load_piece(block, first)

            def rows(part, inner):
                ph = p_high[pl.ds(part * 8, 8)].reshape(512, NB)
                plo = p_low[pl.ds(part * 8, 8)].reshape(512, NB)
                store(multiply(ph, plo), 8, part * 8, at_y * 8 + first)
                return inner

            lax.fori_loop(0, 2, rows, 0)
            return carry

        lax.fori_loop(0, 2, body, 0)

    def z_copy(block, at_y):
        part = pl.ds(at_y * 8, 8)
        return pltpu.make_async_copy(z_buf.at[part], z_out.at[part], z_sem.at[block])

    for zl in range(2):
        wait_p(0, zl)
    for zl_right, zl_left in ((0, 1), (1, 0)):
        start(remote(raw.at[0, zl_right], raw.at[1, zl_right], p_send.at[0, zl_right],
                     p_recv.at[1, zl_right], to_right_x))
        start(remote(raw.at[0, zl_left], raw.at[2, zl_left], p_send.at[1, zl_left],
                     p_recv.at[2, zl_left], to_left_x))
    convert(0)
    own.wait()
    own_times(0)

    wait_x(1, 0)
    start(remote(blocks.at[1, piece(0)], blocks.at[3, piece(0)], x_send.at[2, 0], x_recv.at[3, 0], to_right_y))
    to_sibling(1, 0)
    wait_x(2, 1)
    start(remote(blocks.at[2, piece(1)], blocks.at[3, piece(1)], x_send.at[2, 1], x_recv.at[3, 1], to_left_y))
    to_sibling(2, 1)

    wait_p(1, 0)
    start(remote(raw.at[1, 0], raw.at[3, 0], p_send.at[2, 0], p_recv.at[3, 0], to_right_x))
    wait_p(2, 1)
    start(remote(raw.at[2, 1], raw.at[3, 1], p_send.at[2, 1], p_recv.at[3, 1], to_left_x))
    wait_p(1, 1)
    convert(1)
    own_times(1)
    wait_p(2, 0)
    convert(2)
    own_times(2)
    wait_x(1, 1)
    to_sibling(1, 1)
    wait_x(2, 0)
    to_sibling(2, 0)
    wait_p(3, 0)
    wait_p(3, 1)
    convert(3)
    own_times(3)
    out_copies = [z_copy(0, y)]
    out_copies[-1].start()

    for block, at_y in ((1, left_y), (2, right_y), (3, (y + 2) % 4)):
        if block == 3:
            for q in range(2):
                wait_x(3, q)
                to_sibling(3, q)
        piece_times(block, at_y, lambda k: 4 * core + 2 * k)
        for q in range(2):
            wait_sibling(block, q)
        piece_times(block, at_y, lambda k: 4 * (1 - core) + 2 * k)
        out_copies.append(z_copy(block, at_y))
        out_copies[-1].start()

    for copy in sent:
        copy.wait_send()
    for copy in out_copies:
        copy.wait()


def product(columns, panels):
    dma = pltpu.SemaphoreType.DMA
    return pl.pallas_call(
        product_kernel,
        out_shape=jax.ShapeDtypeStruct((32, 16, 32, 128), F32),
        in_specs=[pl.BlockSpec(memory_space=pl.ANY)] * 2,
        out_specs=pl.BlockSpec(memory_space=pl.ANY),
        scratch_shapes=[
            pltpu.VMEM((4, 2, 2, 2, 32, NB), F32),
            pltpu.VMEM((16, 2, 32, NB), BF16),
            pltpu.VMEM((16, 2, 32, NB), BF16),
            pltpu.VMEM((4, 8, NB, 128), F32),
            pltpu.VMEM((32, 16, 32, 128), F32),
            pltpu.VMEM((NB, 256), BF16),
            pltpu.VMEM((NB, 256), BF16),
            dma, dma((2,)), dma((3, 2)), dma((4, 2)), dma((3, 2)), dma((4, 2)), dma((4, 2)), dma((4, 2)), dma((4,)),
        ],
        compiler_params=pltpu.CompilerParams(
            collective_id=0, has_side_effects=True, vmem_limit_bytes=52 * 2**20
        ),
        cost_estimate=pl.CostEstimate(flops=26_000_000_000, bytes_accessed=40_000_000, transcendentals=0),
        name="product",
    )(columns, panels)


def mix_kernel(
    z_in, mix, columns, shift, turn, out,
    z_buf, mix_high, mix_low, coupled, near, far, own_cols,
    z_sem, col_sem, send_sem, near_sem, far_sem,
):
    mi = lax.axis_index("mult")
    ci = lax.axis_index("chan")
    group, y = ci // 4, ci % 4
    below, above = (group + 7) % 8, (group + 1) % 8
    target = [(mi, below * 4 + 2), (mi, below * 4 + 3)]
    target += [(mi, group * 4 + k) for k in range(4)]
    target += [(mi, above * 4), (mi, above * 4 + 1)]
    outer = jnp.where(y < 2, below, above)

    loads = []
    for t in range(4):
        part = pl.ds(t * 8, 8)
        loads.append(pltpu.make_async_copy(z_in.at[part], z_buf.at[part], z_sem.at[t]))
        loads[-1].start()
    col_load = pltpu.make_async_copy(columns.at[:, pl.ds(mi * 256, 256)], own_cols, col_sem)
    col_load.start()

    barrier = pltpu.get_barrier_semaphore()
    for w in (0, 1, 6, 7):
        pl.semaphore_signal(barrier, inc=1, device_id=target[w], device_id_type=MESH)
    for k in range(4):
        pl.semaphore_signal(barrier, inc=1, device_id=(mi, outer * 4 + k), device_id_type=MESH)
    for k in range(1, 4):
        pl.semaphore_signal(barrier, inc=1, device_id=(mi, group * 4 + (y + k) % 4), device_id_type=MESH)
    pl.semaphore_wait(barrier, 11)

    lane = lax.broadcasted_iota(jnp.int32, (320, 512), 1)
    row = lax.broadcasted_iota(jnp.int32, (320, 512), 0)
    same = (lane % 8) == (row % 8)
    for t in range(4):
        wide = jnp.broadcast_to(mix[t][:, None, :], (40, 8, 512)).reshape(320, 512)
        high, low = split(jnp.where(same, wide, 0.0))
        mix_high[t] = high
        mix_low[t] = low

    def far_copy(w):
        return pltpu.make_async_remote_copy(
            src_ref=coupled.at[w], dst_ref=far.at[y], send_sem=send_sem.at[w], recv_sem=far_sem.at[y],
            device_id=target[w], device_id_type=MESH,
        )

    def near_copy(w):
        return pltpu.make_async_remote_copy(
            src_ref=coupled.at[w], dst_ref=near.at[y], send_sem=send_sem.at[w], recv_sem=near_sem.at[y],
            device_id=target[w], device_id_type=MESH,
        )

    def send_near(w):
        @pl.when(y != w - 2)
        def _():
            near_copy(w).start()

        @pl.when(y == w - 2)
        def _():
            pltpu.make_async_copy(coupled.at[w], near.at[y], near_sem.at[y]).start()

    for t in range(4):
        loads[t].wait()

        def body(k, carry):
            part, first = k // 2, pl.multiple_of((k % 2) * 16, 16)
            tile = z_buf[pl.ds(t * 8, 8), pl.ds(part * 8, 8), pl.ds(first, 16), :]
            both = jnp.concatenate(
                [tile[:, :, :8].reshape(512, 128), tile[:, :, 8:].reshape(512, 128)], axis=1
            )
            high, low = split(both)
            acc = jnp.dot(mix_high[t], high, preferred_element_type=F32)
            acc += jnp.dot(mix_high[t], low, preferred_element_type=F32)
            acc += jnp.dot(mix_low[t], high, preferred_element_type=F32)
            for half in range(2):
                new = acc[:, half * 128:half * 128 + 128].reshape(5, 8, 8, 128)
                at = pl.multiple_of(first + half * 8, 8)
                if t > 0:
                    coupled[pl.ds(t, 4), :, part, pl.ds(at, 8), :] += new[:4]
                    coupled[t + 4, :, part, pl.ds(at, 8), :] = new[4]
                else:
                    coupled[pl.ds(0, 5), :, part, pl.ds(at, 8), :] = new
            return carry

        lax.fori_loop(0, 4, body, 0)
        if t < 2:
            far_copy(t).start()
        if t == 2:
            send_near(2)
    far_copy(6).start()
    far_copy(7).start()
    for w in (3, 4, 5):
        send_near(w)

    col_load.wait()
    for k in range(4):
        pltpu.make_async_copy(coupled.at[0], near.at[k], near_sem.at[k]).wait()
        pltpu.make_async_copy(coupled.at[0], far.at[k], far_sem.at[k]).wait()
        for part in range(2):
            rows = pl.ds(part * 128 + k * 32, 32)
            cols = own_cols[:, rows, :]
            out[:, rows, :] = (
                shift[...] * cols + turn[...] * pltpu.roll(cols, 64, 2) - (near[k, :, part] + far[k, :, part])
            )

    for w in (0, 1, 6, 7):
        far_copy(w).wait_send()
    for w in (2, 3, 4, 5):
        @pl.when(y != w - 2)
        def _():
            near_copy(w).wait_send()


def mix_and_finish(z, mix, columns, shift, turn):
    dma = pltpu.SemaphoreType.DMA
    vmem = pl.BlockSpec(memory_space=pltpu.VMEM)
    anywhere = pl.BlockSpec(memory_space=pl.ANY)
    return pl.pallas_call(
        mix_kernel,
        out_shape=jax.ShapeDtypeStruct((8, 256, 128), F32),
        in_specs=[anywhere, vmem, anywhere, vmem, vmem],
        out_specs=vmem,
        scratch_shapes=[
            pltpu.VMEM((32, 16, 32, 128), F32),
            pltpu.VMEM((4, 320, 512), BF16),
            pltpu.VMEM((4, 320, 512), BF16),
            pltpu.VMEM((8, 8, 2, 32, 128), F32),
            pltpu.VMEM((4, 8, 2, 32, 128), F32),
            pltpu.VMEM((4, 8, 2, 32, 128), F32),
            pltpu.VMEM((8, 256, 128), F32),
            dma((4,)), dma, dma((8,)), dma((4,)), dma((4,)),
        ],
        compiler_params=pltpu.CompilerParams(
            collective_id=1, has_side_effects=True, vmem_limit_bytes=40 * 2**20
        ),
        cost_estimate=pl.CostEstimate(flops=4_000_000_000, bytes_accessed=12_000_000, transcendentals=0),
        name="mix",
    )(z, mix, columns, shift, turn)


def mixing_rows(coefficients, channel_cols, used_slots, lambda_low, lambda_high):
    mi = lax.axis_index("mult")
    ci = lax.axis_index("chan")
    slot_ids = jnp.arange(MAXNZ, dtype=jnp.int32)
    live_slot = slot_ids[None, :] < used_slots[:, None]
    lambda_ids = mi * 2 + jnp.arange(2, dtype=jnp.int32)
    in_range = (lambda_ids >= lambda_low[:, :, None]) & (lambda_ids < lambda_high[:, :, None])
    weights = jnp.where(live_slot[:, :, None] & in_range, coefficients, jnp.zeros_like(coefficients))
    packed = jnp.concatenate([weights, channel_cols[:, :, None].astype(F32)], axis=2)
    whole = lax.all_gather(packed, ("mult", "chan"), axis=0, tiled=False).reshape(4, 32, 8, MAXNZ, 3)
    ring = jnp.concatenate([whole[:, -2:], whole, whole[:, :2]], axis=1)
    group = ci // 4
    near = lax.dynamic_slice_in_dim(ring, group * 4, 8, 1)
    weight = jnp.transpose(near[..., :2], (1, 2, 3, 0, 4)).reshape(64, MAXNZ, 8)
    cols = near[0, :, :, :, 2].reshape(64, MAXNZ) - (group * 32).astype(F32)
    hit = cols[:, :, None] == jnp.arange(32, dtype=jnp.int32).astype(F32)
    mixing = jnp.sum(jnp.where(hit[:, :, :, None], weight[:, :, None, :], 0.0), axis=1)
    parts = [mixing[8 * t:8 * t + 40, 8 * t:8 * t + 8].reshape(40, 64) for t in range(4)]
    return jnp.repeat(jnp.stack(parts), 8, axis=2)


def body(
    columns, panels, coefficients, channel_cols, used_slots, lambda_low, lambda_high, energies, contour
):
    mix = mixing_rows(coefficients, channel_cols, used_slots, lambda_low, lambda_high)
    z = product(columns, panels)
    shift = jnp.broadcast_to((contour[0] - energies)[:, None, None], (8, 1, 128))
    lane = jnp.arange(128, dtype=jnp.int32)
    turn = jnp.where(lane < 64, -contour[1], contour[1])[None, None, :]
    return mix_and_finish(z, mix, columns, shift, turn)


def solution(mesh):
    return jax.shard_map(
        body,
        mesh=mesh,
        in_specs=(
            P("chan", None, None),
            P("mult", None, "chan", None),
            P("chan", None, "mult"),
            P("chan", None),
            P("chan"),
            P("chan", None),
            P("chan", None),
            P("chan"),
            P(),
        ),
        out_specs=P("chan", "mult", None),
        check_vma=False,
    )
```

```python
import jax
import jax.numpy as jnp
from jax import lax
from jax.experimental import pallas as pl
from jax.experimental.pallas import tpu as pltpu
from jax.sharding import PartitionSpec as P

MAXNZ = 16
MESH = pl.DeviceIdType.MESH
F32 = jnp.float32
BF16 = jnp.bfloat16
NB = 1024


def device(z_lo, core, z_hi, x, y):
    return (z_lo * 2 + core, z_hi * 16 + x * 4 + y)


def split(value):
    high = value.astype(BF16)
    return high, (value - high.astype(F32)).astype(BF16)


def swap_halves(value):
    lane = lax.broadcasted_iota(jnp.int32, value.shape, value.ndim - 1)
    rolled = pltpu.roll(value, 64, value.ndim - 1)
    return jnp.where(lane < 64, -rolled, rolled)


def kernel(
    columns, panels, mine, shift, turn, out,
    raw, p_high, p_low, blocks, x_high, x_low, z_first, z_second,
    parts, mix_full, mix_rows, mix_high, mix_low, coupled, near, far,
    own_sem, first_send, p_send, p_recv, x_send, f_send, z_send, x_recv, s_send, s_recv,
    part_send, part_recv, row_send, row_recv, c_send, near_sem, far_sem,
):
    mi = lax.axis_index("mult")
    ci = lax.axis_index("chan")
    z_lo, core, z_hi, x, y = mi // 2, mi % 2, ci // 16, (ci // 4) % 4, ci % 4
    left_x, right_x = (x + 3) % 4, (x + 1) % 4
    left_y, right_y = (y + 3) % 4, (y + 1) % 4
    to_left_x = device(z_lo, core, z_hi, left_x, y)
    to_right_x = device(z_lo, core, z_hi, right_x, y)
    to_left_y = device(z_lo, core, z_hi, x, left_y)
    to_right_y = device(z_lo, core, z_hi, x, right_y)
    sibling = device(z_lo, 1 - core, z_hi, x, y)
    partner = device(1 - z_lo, core, z_hi, x, y)
    full = z_lo == core
    target_x = (x + 2 * core + 3) % 4
    targets = [device(z_hi, x // 2, zh, target_x, y) for zh in range(2)]

    def origin(at_x):
        row_part = 1 - at_x % 2
        from_x = 2 * core + row_part
        from_core = jnp.where((from_x + 1) % 4 == at_x, 1, 0)
        return row_part, from_x, from_core

    _, from_x0, from_core0 = origin(x)
    sources = [device(zl, from_core0, z_lo, from_x0, y) for zl in range(2)]
    spots = [origin(at) for at in (x, left_x, right_x, (x + 2) % 4)]
    first_part, second_part = x % 2, 1 - x % 2

    group = ci // 4
    below, above = (group + 7) % 8, (group + 1) % 8
    owners = [(mi, below * 4 + 2), (mi, below * 4 + 3)]
    owners += [(mi, group * 4 + k) for k in range(4)]
    owners += [(mi, above * 4), (mi, above * 4 + 1)]
    outer = jnp.where(y < 2, below, above)
    outer_spot = jnp.where(y < 2, y + 6, y - 2)
    helpers = [(mi, outer * 4 + k) for k in range(4)]
    mates = [(mi, group * 4 + (y + k) % 4) for k in range(1, 4)]
    others = [((mi + k) % 4, ci) for k in range(1, 4)]

    barrier = pltpu.get_barrier_semaphore()
    peers = [to_left_x, to_right_x] + targets + sources + others + mates + helpers
    peers += [owners[w] for w in (0, 1, 6, 7)]
    for peer in peers:
        pl.semaphore_signal(barrier, inc=1, device_id=peer, device_id_type=MESH)
    pl.semaphore_wait(barrier, len(peers))

    def remote(src, dst, send_sem, recv_sem, peer):
        return pltpu.make_async_remote_copy(
            src_ref=src, dst_ref=dst, send_sem=send_sem, recv_sem=recv_sem,
            device_id=peer, device_id_type=MESH,
        )

    sent = []
    sent_full = []

    def start(copy):
        copy.start()
        sent.append(copy)

    for k in range(2):
        start(remote(panels, raw.at[0, z_lo], first_send.at[k], p_recv.at[0, z_lo], targets[k]))

    def channel(e, s):
        return 4 * core + 2 * e + s

    def own_copies(e):
        copies = []
        for s_right, s_left in ((0, 1), (1, 0)):
            c_right, c_left = channel(e, s_right), channel(e, s_left)
            copies.append(remote(columns.at[c_right], blocks.at[1, c_right],
                                 x_send.at[0, e, s_right], x_recv.at[1, e, s_right], to_right_y))
            copies.append(remote(columns.at[c_left], blocks.at[2, c_left],
                                 x_send.at[1, e, s_left], x_recv.at[2, e, s_left], to_left_y))
        return copies

    common, extra = own_copies(0), own_copies(1)
    for copy in common[:2]:
        start(copy)

    @pl.when(full)
    def _():
        for copy in extra[:2]:
            copy.start()

    for copy in common[2:]:
        start(copy)

    @pl.when(full)
    def _():
        for copy in extra[2:]:
            copy.start()

    sent_full += extra

    own = pltpu.make_async_copy(columns, blocks.at[0], own_sem)
    own.start()
    for k in range(3):
        start(remote(mine, parts.at[2 - k], part_send.at[k], part_recv.at[2 - k], others[k]))

    def wait_p(slot, zl):
        ref = raw.at[slot, zl]
        remote(ref, ref, p_send.at[0, zl], p_recv.at[slot, zl], to_right_x).wait_recv()

    def forward_p(zl):
        slot, peer = (1, to_right_x) if zl == 0 else (2, to_left_x)
        start(remote(raw.at[slot, zl], raw.at[3, zl], p_send.at[2, zl], p_recv.at[3, zl], peer))

    def wait_x(b, e, s):
        ref = blocks.at[b, channel(e, s)]
        remote(ref, ref, x_send.at[0, e, s], x_recv.at[b, e, s], to_right_y).wait_recv()

    def forward_x(e, s):
        c = channel(e, s)
        b, peer = (1, to_right_y) if s == 0 else (2, to_left_y)
        return remote(blocks.at[b, c], blocks.at[3, c], f_send.at[e, s], x_recv.at[3, e, s], peer)

    def to_partner(b, s):
        ref = blocks.at[b, channel(1, s)]
        return remote(ref, ref, z_send.at[b, s], x_recv.at[b, 1, s], partner)

    def to_sibling(b, e, s):
        ref = blocks.at[b, channel(e, s)]
        start(remote(ref, ref, s_send.at[b, e, s], s_recv.at[b, e, s], sibling))

    def wait_sibling(b):
        for e in range(2):
            for s in range(2):
                ref = blocks.at[b, 4 * (1 - core) + 2 * e + s]
                remote(ref, ref, s_send.at[b, e, s], s_recv.at[b, e, s], sibling).wait_recv()

    def take_extra(pairs, onward):
        @pl.when(full)
        def _():
            for b, s in pairs:
                wait_x(b, 1, s)
                if onward:
                    forward_x(1, s).start()
                to_partner(b, s).start()

        for b, s in pairs:
            if onward:
                sent_full.append(forward_x(1, s))
            sent_full.append(to_partner(b, s))

    def pass_extra(pairs):
        @pl.when(jnp.logical_not(full))
        def _():
            for b, s in pairs:
                wait_x(b, 1, s)

        for b, s in pairs:
            to_sibling(b, 1, s)

    def convert_p(slot):
        row_part, _, from_core = spots[slot]
        for zl in range(2):
            for order in range(2):
                at = row_part * 8 + 4 * zl + 2 * from_core + order
                for ri in range(2):
                    high, low = split(raw[slot, zl, order, ri])
                    p_high[at, ri] = high
                    p_low[at, ri] = low

    def convert_x(b, first, count):
        def step(k, carry):
            piece = first + k
            both = jnp.concatenate([blocks[b, 2 * piece], blocks[b, 2 * piece + 1]], axis=1)
            high, low = split(both)
            x_high[b * 4 + piece] = high
            x_low[b * 4 + piece] = low
            return carry

        lax.fori_loop(0, count, step, 0)

    def multiply(ph, plo, piece):
        acc = jnp.dot(ph, x_high[piece], preferred_element_type=F32)
        acc += jnp.dot(plo, x_high[piece], preferred_element_type=F32)
        acc += jnp.dot(ph, x_low[piece], preferred_element_type=F32)
        return acc

    def store(ref, acc, count, at, chan):
        acc = acc.reshape(count, 2, 32, 256)
        for half in range(2):
            part = acc[..., half * 128:half * 128 + 128]
            ref[chan + half, pl.ds(at, count)] = part[:, 0] + swap_halves(part[:, 1])

    def unit_slot(slot, b):
        row_part, _, from_core = spots[slot]
        ats = [4 * zl + 2 * from_core for zl in range(2)]

        def step(k, carry):
            ph = jnp.concatenate([p_high[pl.ds(row_part * 8 + at, 2)] for at in ats], axis=0)
            plo = jnp.concatenate([p_low[pl.ds(row_part * 8 + at, 2)] for at in ats], axis=0)
            acc = multiply(ph.reshape(256, NB), plo.reshape(256, NB), b * 4 + k)
            for zl in range(2):
                store(z_second, acc[zl * 128:zl * 128 + 128], 2, ats[zl], b * 8 + 2 * k)
            return carry

        lax.fori_loop(0, 4, step, 0)

    def unit_first(b):
        def step(k, carry):
            ph = p_high[pl.ds(first_part * 8, 8)].reshape(512, NB)
            plo = p_low[pl.ds(first_part * 8, 8)].reshape(512, NB)
            store(z_first, multiply(ph, plo, b * 4 + k), 8, 0, 2 * k)
            return carry

        lax.fori_loop(0, 4, step, 0)

    at_y = [y, left_y, right_y, (y + 2) % 4]

    def mix(ref, base, b, part):
        t = at_y[b]

        def step(k, carry):
            first = pl.multiple_of(k * 16, 16)
            tile = ref[pl.ds(base, 8), :, pl.ds(first, 16), :]
            both = jnp.concatenate(
                [tile[:, :, :8].reshape(512, 128), tile[:, :, 8:].reshape(512, 128)], axis=1
            )
            high, low = split(both)
            acc = jnp.dot(mix_high[t], high, preferred_element_type=F32)
            acc += jnp.dot(mix_high[t], low, preferred_element_type=F32)
            acc += jnp.dot(mix_low[t], high, preferred_element_type=F32)
            for half in range(2):
                new = acc[:, half * 128:half * 128 + 128].reshape(5, 8, 8, 128)
                at = pl.multiple_of(first + half * 8, 8)
                coupled[part, pl.ds(t, 5), :, pl.ds(at, 8), :] += new
            return carry

        lax.fori_loop(0, 2, step, 0)

    def far_copy(part, w):
        return remote(coupled.at[part, w], far.at[part, y], c_send.at[part, w], far_sem.at[part, y], owners[w])

    def near_copy(part, w):
        return remote(coupled.at[part, w], near.at[part, y], c_send.at[part, w], near_sem.at[part, y], owners[w])

    def send_coupled(part):
        for w in (0, 1, 6, 7):
            far_copy(part, w).start()
        for w in (2, 3, 4, 5):
            @pl.when(y != w - 2)
            def _():
                near_copy(part, w).start()

        pltpu.make_async_copy(coupled.at[part, y + 2], near.at[part, y], near_sem.at[part, y]).start()

    def build_mix():
        wide_row = lax.broadcasted_iota(jnp.int32, (128, 512), 0)
        wide_lane = lax.broadcasted_iota(jnp.int32, (128, 512), 1)
        widen = jnp.where(wide_lane // 8 == wide_row, 1.0, 0.0).astype(BF16)
        lane = lax.broadcasted_iota(jnp.int32, (320, 512), 1)
        row = lax.broadcasted_iota(jnp.int32, (320, 512), 0)
        same = (lane % 8) == (row % 8)
        for t in range(4):
            rows = jnp.concatenate([mix_rows[t + k, 8 * (4 - k):8 * (4 - k) + 8] for k in range(5)], axis=0)
            for ref, value in zip((mix_high, mix_low), split(rows)):
                wide = jnp.dot(value, widen, preferred_element_type=F32)
                wide = jnp.broadcast_to(wide[:, None, :], (40, 8, 512)).reshape(320, 512)
                ref[t] = jnp.where(same, wide, 0.0).astype(BF16)

    coupled[...] = jnp.zeros_like(coupled)
    for k in range(3):
        remote(mine, parts.at[k], part_send.at[k], part_recv.at[k], others[k]).wait_recv()
    mix_full[...] = mine[...] + parts[0] + parts[1] + parts[2]
    mix_rows[y + 2] = mix_full[...]
    for k in range(3):
        start(remote(mix_full, mix_rows.at[y + 2], row_send.at[k], row_recv.at[y + 2], mates[k]))
    for k in range(4):
        start(remote(mix_full, mix_rows.at[outer_spot], row_send.at[3 + k], row_recv.at[outer_spot], helpers[k]))
    own.wait()
    convert_x(0, 0, 4)

    for zl in range(2):
        wait_p(0, zl)
    for zl_right, zl_left in ((0, 1), (1, 0)):
        start(remote(raw.at[0, zl_right], raw.at[1, zl_right], p_send.at[0, zl_right],
                     p_recv.at[1, zl_right], to_right_x))
        start(remote(raw.at[0, zl_left], raw.at[2, zl_left], p_send.at[1, zl_left],
                     p_recv.at[2, zl_left], to_left_x))
    convert_p(0)
    unit_slot(0, 0)

    early, late = ((1, 0), (2, 1)), ((1, 1), (2, 0))
    for b, s in early:
        wait_x(b, 0, s)
        start(forward_x(0, s))
        to_sibling(b, 0, s)
    take_extra(early, True)
    for zl in range(2):
        wait_p(1 + zl, zl)
        forward_p(zl)

    for w in range(8):
        @pl.when(w != y + 2)
        def _():
            remote(mix_full, mix_rows.at[w], row_send.at[0], row_recv.at[w], mates[0]).wait_recv()

    build_mix()

    wait_p(1, 1)
    convert_p(1)
    wait_p(2, 0)
    convert_p(2)
    unit_first(0)
    mix(z_first, 0, 0, first_part)
    for b, s in late:
        wait_x(b, 0, s)
        to_sibling(b, 0, s)
    take_extra(late, False)
    pass_extra(early)
    pass_extra(late)
    for b in (1, 2):
        convert_x(b, 2 * core, 2)
        wait_sibling(b)
        convert_x(b, 2 * (1 - core), 2)
        unit_slot(0, b)
        unit_first(b)
        mix(z_first, 0, b, first_part)

    last = ((3, 0), (3, 1))
    for b, s in last:
        wait_x(b, 0, s)
        to_sibling(b, 0, s)
    take_extra(last, False)
    wait_p(3, 0)
    wait_p(3, 1)
    convert_p(3)
    unit_slot(3, 0)
    mix(z_second, 0, 0, second_part)
    pass_extra(last)
    convert_x(3, 2 * core, 2)
    wait_sibling(3)
    convert_x(3, 2 * (1 - core), 2)
    unit_first(3)
    mix(z_first, 0, 3, first_part)
    send_coupled(first_part)
    for b in (1, 2):
        unit_slot(3, b)
        mix(z_second, b * 8, b, second_part)
    unit_slot(0, 3)
    unit_slot(3, 3)
    mix(z_second, 24, 3, second_part)
    send_coupled(second_part)

    for part in (first_part, second_part):
        for k in range(4):
            pltpu.make_async_copy(coupled.at[0, 0], near.at[part, k], near_sem.at[part, k]).wait()
            pltpu.make_async_copy(coupled.at[0, 0], far.at[part, k], far_sem.at[part, k]).wait()
            at = part * 128 + k * 32
            cols = blocks[0, :, pl.ds(pl.multiple_of(mi * 256 + at, 32), 32), :]
            out[:, pl.ds(pl.multiple_of(at, 32), 32), :] = (
                shift[...] * cols + turn[...] * pltpu.roll(cols, 64, 2) - (near[part, k] + far[part, k])
            )

    for copy in sent:
        copy.wait_send()

    @pl.when(full)
    def _():
        for copy in sent_full:
            copy.wait_send()

    for part in range(2):
        for w in (0, 1, 6, 7):
            far_copy(part, w).wait_send()
        for w in (2, 3, 4, 5):
            @pl.when(y != w - 2)
            def _():
                near_copy(part, w).wait_send()


def filter_step(columns, panels, mine, shift, turn):
    dma = pltpu.SemaphoreType.DMA
    vmem = pl.BlockSpec(memory_space=pltpu.VMEM)
    anywhere = pl.BlockSpec(memory_space=pl.ANY)
    return pl.pallas_call(
        kernel,
        out_shape=jax.ShapeDtypeStruct((8, 256, 128), F32),
        in_specs=[anywhere, anywhere, vmem, vmem, vmem],
        out_specs=vmem,
        scratch_shapes=[
            pltpu.VMEM((4, 2, 2, 2, 32, NB), F32),
            pltpu.VMEM((16, 2, 32, NB), BF16),
            pltpu.VMEM((16, 2, 32, NB), BF16),
            pltpu.VMEM((4, 8, NB, 128), F32),
            pltpu.VMEM((16, NB, 256), BF16),
            pltpu.VMEM((16, NB, 256), BF16),
            pltpu.VMEM((8, 8, 32, 128), F32),
            pltpu.VMEM((32, 8, 32, 128), F32),
            pltpu.VMEM((3, 40, 128), F32),
            pltpu.VMEM((40, 128), F32),
            pltpu.VMEM((8, 40, 128), F32),
            pltpu.VMEM((4, 320, 512), BF16),
            pltpu.VMEM((4, 320, 512), BF16),
            pltpu.VMEM((2, 8, 8, 32, 128), F32),
            pltpu.VMEM((2, 4, 8, 32, 128), F32),
            pltpu.VMEM((2, 4, 8, 32, 128), F32),
            dma, dma((2,)), dma((3, 2)), dma((4, 2)),
            dma((2, 2, 2)), dma((2, 2)), dma((4, 2)), dma((4, 2, 2)), dma((4, 2, 2)), dma((4, 2, 2)),
            dma((3,)), dma((3,)), dma((7,)), dma((8,)), dma((2, 8)), dma((2, 4)), dma((2, 4)),
        ],
        compiler_params=pltpu.CompilerParams(
            collective_id=0, has_side_effects=True, vmem_limit_bytes=60 * 2**20
        ),
        cost_estimate=pl.CostEstimate(flops=30_000_000_000, bytes_accessed=40_000_000, transcendentals=0),
        name="filter_step",
    )(columns, panels, mine, shift, turn)


def own_mixing(coefficients, channel_cols, used_slots, lambda_low, lambda_high):
    mi = lax.axis_index("mult")
    ci = lax.axis_index("chan")
    lane = jnp.arange(128, dtype=jnp.int32)
    order = lane % 8
    slot_ids = jnp.arange(MAXNZ, dtype=jnp.int32)
    live_slot = slot_ids[None, :] < used_slots[:, None]
    keep = live_slot[:, :, None] & (order >= lambda_low[:, :, None]) & (order < lambda_high[:, :, None])
    keep &= (order // 2 == mi) & (lane < 64)
    value = jnp.where(order % 2 == 0, coefficients[:, :, :1], coefficients[:, :, 1:])
    weights = jnp.where(keep, value, 0.0)
    local = channel_cols - (ci - 2) * 8
    distance = jnp.arange(5, dtype=jnp.int32)
    hit = local[None, :, :, None] == distance[:, None, None, None] * 8 + lane // 8
    return jnp.sum(jnp.where(hit, weights[None], 0.0), axis=2).reshape(40, 128)


def body(
    columns, panels, coefficients, channel_cols, used_slots, lambda_low, lambda_high, energies, contour
):
    mine = own_mixing(coefficients, channel_cols, used_slots, lambda_low, lambda_high)
    shift = jnp.broadcast_to((contour[0] - energies)[:, None, None], (8, 1, 128))
    lane = jnp.arange(128, dtype=jnp.int32)
    turn = jnp.where(lane < 64, -contour[1], contour[1])[None, None, :]
    return filter_step(columns, panels, mine, shift, turn)


def solution(mesh):
    return jax.shard_map(
        body,
        mesh=mesh,
        in_specs=(
            P("chan", None, None),
            P("mult", None, "chan", None),
            P("chan", None, "mult"),
            P("chan", None),
            P("chan"),
            P("chan", None),
            P("chan", None),
            P("chan"),
            P(),
        ),
        out_specs=P("chan", "mult", None),
        check_vma=False,
    )
```

```python
import jax
import jax.numpy as jnp
from jax import lax
from jax.experimental import pallas as pl
from jax.experimental.pallas import tpu as pltpu
from jax.sharding import PartitionSpec as P

MAXNZ = 16
MESH = pl.DeviceIdType.MESH
F32 = jnp.float32
BF16 = jnp.bfloat16
NB = 1024


def device(z_lo, core, z_hi, x, y):
    return (z_lo * 2 + core, z_hi * 16 + x * 4 + y)


def split(value):
    high = value.astype(BF16)
    return high, (value - high.astype(F32)).astype(BF16)


def swap_halves(value):
    lane = lax.broadcasted_iota(jnp.int32, value.shape, value.ndim - 1)
    rolled = pltpu.roll(value, 64, value.ndim - 1)
    return jnp.where(lane < 64, -rolled, rolled)


def own_mixing(coefficients, channel_cols, lambda_low, lambda_high, used_slots, mine):
    mi = lax.axis_index("mult")
    ci = lax.axis_index("chan")
    lane = lax.broadcasted_iota(jnp.int32, (8, 128), 1)
    row = lax.broadcasted_iota(jnp.int32, (8, 128), 0)
    order = lane % 8
    used = jnp.zeros((8, 128), jnp.int32)
    for i in range(8):
        used = jnp.where(row == i, used_slots[i], used)
    own_order = (order // 2 == mi) & (lane < 64)

    def wide(ref_value, s):
        return jnp.broadcast_to(ref_value[:, s:s + 1], (8, 128))

    even, odd = coefficients[0], coefficients[1]
    low, high, cols = lambda_low[...], lambda_high[...], channel_cols[...]
    sums = [jnp.zeros((8, 128), F32) for _ in range(5)]
    for s in range(MAXNZ):
        value = jnp.where(order % 2 == 0, wide(even, s), wide(odd, s))
        keep = own_order & (used > s) & (order >= wide(low, s)) & (order < wide(high, s))
        value = jnp.where(keep, value, 0.0)
        local = wide(cols, s) - (ci - 2) * 8 - lane // 8
        for d in range(5):
            sums[d] += jnp.where(local == d * 8, value, 0.0)
    mine[...] = jnp.concatenate(sums, axis=0)


def kernel(
    columns, panels, coefficients, channel_cols, lambda_low, lambda_high, used_slots, energies, contour, out,
    raw, p_high, p_low, blocks, x_high, x_low, z_first, z_second,
    mine, parts, mix_rows, mix_high, mix_low, coupled, near, far,
    own_sem, first_send, p_send, p_recv, x_send, f_send, z_send, x_recv, s_send, s_recv,
    part_send, part_recv, row_send, row_recv, pair_send, pair_recv, near_send, near_sem, far_send, far_sem,
):
    mi = lax.axis_index("mult")
    ci = lax.axis_index("chan")
    z_lo, core, z_hi, x, y = mi // 2, mi % 2, ci // 16, (ci // 4) % 4, ci % 4
    left_x, right_x = (x + 3) % 4, (x + 1) % 4
    left_y, right_y = (y + 3) % 4, (y + 1) % 4
    to_left_x = device(z_lo, core, z_hi, left_x, y)
    to_right_x = device(z_lo, core, z_hi, right_x, y)
    to_left_y = device(z_lo, core, z_hi, x, left_y)
    to_right_y = device(z_lo, core, z_hi, x, right_y)
    sibling = device(z_lo, 1 - core, z_hi, x, y)
    partner = device(1 - z_lo, core, z_hi, x, y)
    full = z_lo == core
    target_x = (x + 2 * core + 3) % 4
    targets = [device(z_hi, x // 2, zh, target_x, y) for zh in range(2)]

    def origin(at_x):
        row_part = 1 - at_x % 2
        from_x = 2 * core + row_part
        from_core = jnp.where((from_x + 1) % 4 == at_x, 1, 0)
        return row_part, from_x, from_core

    _, from_x0, from_core0 = origin(x)
    sources = [device(zl, from_core0, z_lo, from_x0, y) for zl in range(2)]
    spots = [origin(at) for at in (x, left_x, right_x, (x + 2) % 4)]
    first_part, second_part = x % 2, 1 - x % 2

    group = ci // 4
    below = (mi, (group + 7) % 8 * 4 + y)
    above = (mi, (group + 1) % 8 * 4 + y)
    mates = [(mi, group * 4 + (y + k) % 4) for k in range(1, 4)]
    others = [((mi + k) % 4, ci) for k in range(1, 4)]

    barrier = pltpu.get_barrier_semaphore()
    peers = [to_left_x, to_right_x, below, above] + targets + sources + others + mates
    for peer in peers:
        pl.semaphore_signal(barrier, inc=1, device_id=peer, device_id_type=MESH)

    own = pltpu.make_async_copy(columns, blocks.at[0], own_sem)
    own.start()
    own_mixing(coefficients, channel_cols, lambda_low, lambda_high, used_slots, mine)
    coupled[...] = jnp.zeros_like(coupled)
    pl.semaphore_wait(barrier, len(peers))

    def remote(src, dst, send_sem, recv_sem, peer):
        return pltpu.make_async_remote_copy(
            src_ref=src, dst_ref=dst, send_sem=send_sem, recv_sem=recv_sem,
            device_id=peer, device_id_type=MESH,
        )

    sent = []
    sent_full = []

    def start(copy):
        copy.start()
        sent.append(copy)

    for k in range(2):
        start(remote(panels, raw.at[0, z_lo], first_send.at[k], p_recv.at[0, z_lo], targets[k]))

    def channel(e, s):
        return 4 * core + 2 * e + s

    def own_copies(e):
        copies = []
        for s_right, s_left in ((0, 1), (1, 0)):
            c_right, c_left = channel(e, s_right), channel(e, s_left)
            copies.append(remote(columns.at[c_right], blocks.at[1, c_right],
                                 x_send.at[0, e, s_right], x_recv.at[1, e, s_right], to_right_y))
            copies.append(remote(columns.at[c_left], blocks.at[2, c_left],
                                 x_send.at[1, e, s_left], x_recv.at[2, e, s_left], to_left_y))
        return copies

    common, extra = own_copies(0), own_copies(1)

    @pl.when(full)
    def _():
        for copy in extra[:2]:
            copy.start()

    for copy in common[:2]:
        start(copy)

    @pl.when(full)
    def _():
        for copy in extra[2:]:
            copy.start()

    for copy in common[2:]:
        start(copy)
    sent_full += extra
    for k in range(3):
        start(remote(mine, parts.at[2 - k], part_send.at[k], part_recv.at[2 - k], others[k]))

    def wait_p(slot, zl):
        ref = raw.at[slot, zl]
        remote(ref, ref, p_send.at[0, zl], p_recv.at[slot, zl], to_right_x).wait_recv()

    def forward_p(zl):
        slot, peer = (1, to_right_x) if zl == 0 else (2, to_left_x)
        start(remote(raw.at[slot, zl], raw.at[3, zl], p_send.at[2, zl], p_recv.at[3, zl], peer))

    def wait_x(b, e, s):
        ref = blocks.at[b, channel(e, s)]
        remote(ref, ref, x_send.at[0, e, s], x_recv.at[b, e, s], to_right_y).wait_recv()

    def forward_x(e, s):
        c = channel(e, s)
        b, peer = (1, to_right_y) if s == 0 else (2, to_left_y)
        return remote(blocks.at[b, c], blocks.at[3, c], f_send.at[e, s], x_recv.at[3, e, s], peer)

    def to_partner(b, s):
        ref = blocks.at[b, channel(1, s)]
        return remote(ref, ref, z_send.at[b, s], x_recv.at[b, 1, s], partner)

    def to_sibling(b, e, s):
        ref = blocks.at[b, channel(e, s)]
        start(remote(ref, ref, s_send.at[b, e, s], s_recv.at[b, e, s], sibling))

    def wait_sibling(b):
        for e in range(2):
            for s in range(2):
                ref = blocks.at[b, 4 * (1 - core) + 2 * e + s]
                remote(ref, ref, s_send.at[b, e, s], s_recv.at[b, e, s], sibling).wait_recv()

    def take_extra(pairs, onward):
        @pl.when(full)
        def _():
            for b, s in pairs:
                wait_x(b, 1, s)
                if onward:
                    forward_x(1, s).start()
                to_partner(b, s).start()

        for b, s in pairs:
            if onward:
                sent_full.append(forward_x(1, s))
            sent_full.append(to_partner(b, s))

    def pass_extra(pairs):
        @pl.when(jnp.logical_not(full))
        def _():
            for b, s in pairs:
                wait_x(b, 1, s)

        for b, s in pairs:
            to_sibling(b, 1, s)

    def convert_p(slot):
        row_part, _, from_core = spots[slot]
        for zl in range(2):
            for order in range(2):
                at = row_part * 8 + 4 * zl + 2 * from_core + order
                for ri in range(2):
                    high, low = split(raw[slot, zl, order, ri])
                    p_high[at, ri] = high
                    p_low[at, ri] = low

    def convert_x(b, first, count):
        def step(k, carry):
            piece = first + k
            both = jnp.concatenate([blocks[b, 2 * piece], blocks[b, 2 * piece + 1]], axis=1)
            high, low = split(both)
            x_high[b * 4 + piece] = high
            x_low[b * 4 + piece] = low
            return carry

        lax.fori_loop(0, count, step, 0)

    def multiply(ph, plo, piece):
        acc = jnp.dot(ph, x_high[piece], preferred_element_type=F32)
        acc += jnp.dot(plo, x_high[piece], preferred_element_type=F32)
        acc += jnp.dot(ph, x_low[piece], preferred_element_type=F32)
        return acc

    def store(ref, acc, count, at, chan):
        acc = acc.reshape(count, 2, 32, 256)
        for half in range(2):
            part = acc[..., half * 128:half * 128 + 128]
            ref[chan + half, pl.ds(at, count)] = part[:, 0] + swap_halves(part[:, 1])

    def unit_slot(slot, b):
        row_part, _, from_core = spots[slot]
        ats = [4 * zl + 2 * from_core for zl in range(2)]

        def step(k, carry):
            ph = jnp.concatenate([p_high[pl.ds(row_part * 8 + at, 2)] for at in ats], axis=0)
            plo = jnp.concatenate([p_low[pl.ds(row_part * 8 + at, 2)] for at in ats], axis=0)
            acc = multiply(ph.reshape(256, NB), plo.reshape(256, NB), b * 4 + k)
            for zl in range(2):
                store(z_second, acc[zl * 128:zl * 128 + 128], 2, ats[zl], b * 8 + 2 * k)
            return carry

        lax.fori_loop(0, 4, step, 0)

    def unit_first(b):
        def step(k, carry):
            ph = p_high[pl.ds(first_part * 8, 8)].reshape(512, NB)
            plo = p_low[pl.ds(first_part * 8, 8)].reshape(512, NB)
            store(z_first, multiply(ph, plo, b * 4 + k), 8, 0, 2 * k)
            return carry

        lax.fori_loop(0, 4, step, 0)

    at_y = [y, left_y, right_y, (y + 2) % 4]

    def mix(ref, base, b, part):
        t = at_y[b]

        def step(k, carry):
            first = pl.multiple_of(k * 16, 16)
            tile = ref[pl.ds(base, 8), :, pl.ds(first, 16), :]
            both = jnp.concatenate(
                [tile[:, :, :8].reshape(512, 128), tile[:, :, 8:].reshape(512, 128)], axis=1
            )
            high, low = split(both)
            acc = jnp.dot(mix_high[t], high, preferred_element_type=F32)
            acc += jnp.dot(mix_high[t], low, preferred_element_type=F32)
            acc += jnp.dot(mix_low[t], high, preferred_element_type=F32)
            for half in range(2):
                new = acc[:, half * 128:half * 128 + 128].reshape(5, 8, 8, 128)
                at = pl.multiple_of(first + half * 8, 8)
                coupled[part, pl.ds(t, 5), :, pl.ds(at, 8), :] += new
            return carry

        lax.fori_loop(0, 2, step, 0)

    def far_copies(part):
        return [
            remote(coupled.at[part, pl.ds(0, 2)], far.at[part, 1], far_send.at[part, 0], far_sem.at[part, 1], below),
            remote(coupled.at[part, pl.ds(6, 2)], far.at[part, 0], far_send.at[part, 1], far_sem.at[part, 0], above),
        ]

    def near_copies(part):
        return [
            remote(coupled.at[part, 2 + (y + k) % 4], near.at[part, y], near_send.at[part, k - 1],
                   near_sem.at[part, y], mates[k - 1])
            for k in range(1, 4)
        ]

    def send_far(part):
        for copy in far_copies(part):
            start(copy)

    def send_near(part):
        for k in range(2):
            ref = far.at[part, k]
            remote(ref, ref, far_send.at[part, k], far_sem.at[part, k], below).wait_recv()
            coupled[part, pl.ds(2 + 2 * k, 2)] += far[part, k]
        for copy in near_copies(part):
            start(copy)
        near[part, y] = coupled[part, 2 + y]

    def finish(part):
        for k in range(1, 4):
            ref = near.at[part, (y + k) % 4]
            remote(ref, ref, near_send.at[part, 0], near_sem.at[part, (y + k) % 4], mates[0]).wait_recv()
        lane = lax.broadcasted_iota(jnp.int32, (32, 128), 1)
        turn = jnp.where(lane < 64, -contour[1], contour[1])
        for k in range(4):
            at = part * 128 + k * 32
            for i in range(8):
                cols = blocks[0, i, pl.ds(pl.multiple_of(mi * 256 + at, 32), 32), :]
                out[i, pl.ds(pl.multiple_of(at, 32), 32), :] = (
                    (contour[0] - energies[i]) * cols + turn * pltpu.roll(cols, 64, 1) - near[part, k, i]
                )

    def build_mix():
        wide_row = lax.broadcasted_iota(jnp.int32, (128, 512), 0)
        wide_lane = lax.broadcasted_iota(jnp.int32, (128, 512), 1)
        widen = jnp.where(wide_lane // 8 == wide_row, 1.0, 0.0).astype(BF16)
        lane = lax.broadcasted_iota(jnp.int32, (320, 512), 1)
        row = lax.broadcasted_iota(jnp.int32, (320, 512), 0)
        same = (lane % 8) == (row % 8)
        for t in range(4):
            rows = jnp.concatenate([mix_rows[t + k, 8 * (4 - k):8 * (4 - k) + 8] for k in range(5)], axis=0)
            for ref, value in zip((mix_high, mix_low), split(rows)):
                wide = jnp.dot(value, widen, preferred_element_type=F32)
                wide = jnp.broadcast_to(wide[:, None, :], (40, 8, 512)).reshape(320, 512)
                ref[t] = jnp.where(same, wide, 0.0).astype(BF16)

    for k in range(3):
        remote(mine, parts.at[k], part_send.at[k], part_recv.at[k], others[k]).wait_recv()
    mix_rows[y + 2] = mine[...] + parts[0] + parts[1] + parts[2]
    for k in range(3):
        start(remote(mix_rows.at[y + 2], mix_rows.at[y + 2], row_send.at[k], row_recv.at[y], mates[k]))
    own.wait()
    convert_x(0, 0, 4)

    for zl in range(2):
        wait_p(0, zl)
    for zl_right, zl_left in ((0, 1), (1, 0)):
        start(remote(raw.at[0, zl_right], raw.at[1, zl_right], p_send.at[0, zl_right],
                     p_recv.at[1, zl_right], to_right_x))
        start(remote(raw.at[0, zl_left], raw.at[2, zl_left], p_send.at[1, zl_left],
                     p_recv.at[2, zl_left], to_left_x))
    for k in range(1, 4):
        ref = mix_rows.at[2 + (y + k) % 4]
        remote(ref, ref, row_send.at[0], row_recv.at[(y + k) % 4], mates[0]).wait_recv()
    start(remote(mix_rows.at[pl.ds(2, 2)], mix_rows.at[pl.ds(6, 2)], pair_send.at[0], pair_recv.at[0], below))
    start(remote(mix_rows.at[pl.ds(4, 2)], mix_rows.at[pl.ds(0, 2)], pair_send.at[1], pair_recv.at[1], above))
    convert_p(0)
    unit_slot(0, 0)

    early, late, last = ((1, 0), (2, 1)), ((1, 1), (2, 0)), ((3, 0), (3, 1))
    take_extra(early, True)
    for b, s in early:
        wait_x(b, 0, s)
        start(forward_x(0, s))
        to_sibling(b, 0, s)
    for k in range(2):
        ref = mix_rows.at[pl.ds(6 - 6 * k, 2)]
        remote(ref, ref, pair_send.at[k], pair_recv.at[k], below).wait_recv()
    for zl in range(2):
        wait_p(1 + zl, zl)
        forward_p(zl)
    build_mix()
    take_extra(late, False)
    for b, s in late:
        wait_x(b, 0, s)
        to_sibling(b, 0, s)
    wait_p(1, 1)
    convert_p(1)
    wait_p(2, 0)
    convert_p(2)
    unit_first(0)
    pass_extra(early)
    pass_extra(late)
    mix(z_first, 0, 0, first_part)
    for b in (1, 2):
        convert_x(b, 2 * core, 2)
    for b in (1, 2):
        wait_sibling(b)
        convert_x(b, 2 * (1 - core), 2)
        unit_slot(0, b)
    take_extra(last, False)
    for b, s in last:
        wait_x(b, 0, s)
        to_sibling(b, 0, s)
    unit_first(1)
    mix(z_first, 0, 1, first_part)
    pass_extra(last)
    unit_first(2)
    mix(z_first, 0, 2, first_part)
    convert_x(3, 2 * core, 2)
    wait_sibling(3)
    convert_x(3, 2 * (1 - core), 2)
    unit_first(3)
    mix(z_first, 0, 3, first_part)
    send_far(first_part)
    wait_p(3, 0)
    wait_p(3, 1)
    convert_p(3)
    unit_slot(0, 3)
    for b in range(4):
        unit_slot(3, b)
        mix(z_second, b * 8, b, second_part)
    send_far(second_part)
    send_near(second_part)
    send_near(first_part)
    finish(second_part)
    finish(first_part)

    for copy in sent:
        copy.wait_send()

    @pl.when(full)
    def _():
        for copy in sent_full:
            copy.wait_send()


def filter_step(*operands):
    dma = pltpu.SemaphoreType.DMA
    vmem = pl.BlockSpec(memory_space=pltpu.VMEM)
    smem = pl.BlockSpec(memory_space=pltpu.SMEM)
    anywhere = pl.BlockSpec(memory_space=pl.ANY)
    return pl.pallas_call(
        kernel,
        out_shape=jax.ShapeDtypeStruct((8, 256, 128), F32),
        in_specs=[anywhere] * 2 + [vmem] * 4 + [smem] * 3,
        out_specs=vmem,
        scratch_shapes=[
            pltpu.VMEM((4, 2, 2, 2, 32, NB), F32),
            pltpu.VMEM((16, 2, 32, NB), BF16),
            pltpu.VMEM((16, 2, 32, NB), BF16),
            pltpu.VMEM((4, 8, NB, 128), F32),
            pltpu.VMEM((16, NB, 256), BF16),
            pltpu.VMEM((16, NB, 256), BF16),
            pltpu.VMEM((8, 8, 32, 128), F32),
            pltpu.VMEM((32, 8, 32, 128), F32),
            pltpu.VMEM((40, 128), F32),
            pltpu.VMEM((3, 40, 128), F32),
            pltpu.VMEM((8, 40, 128), F32),
            pltpu.VMEM((4, 320, 512), BF16),
            pltpu.VMEM((4, 320, 512), BF16),
            pltpu.VMEM((2, 8, 8, 32, 128), F32),
            pltpu.VMEM((2, 4, 8, 32, 128), F32),
            pltpu.VMEM((2, 2, 2, 8, 32, 128), F32),
            dma, dma((2,)), dma((3, 2)), dma((4, 2)),
            dma((2, 2, 2)), dma((2, 2)), dma((4, 2)), dma((4, 2, 2)), dma((4, 2, 2)), dma((4, 2, 2)),
            dma((3,)), dma((3,)), dma((3,)), dma((4,)), dma((2,)), dma((2,)),
            dma((2, 3)), dma((2, 4)), dma((2, 2)), dma((2, 2)),
        ],
        compiler_params=pltpu.CompilerParams(
            collective_id=0, has_side_effects=True, vmem_limit_bytes=60 * 2**20
        ),
        cost_estimate=pl.CostEstimate(flops=30_000_000_000, bytes_accessed=40_000_000, transcendentals=0),
        name="filter_step",
    )(*operands)


def body(
    columns, panels, coefficients, channel_cols, used_slots, lambda_low, lambda_high, energies, contour
):
    return filter_step(
        columns, panels, jnp.transpose(coefficients, (2, 0, 1)), channel_cols, lambda_low, lambda_high,
        used_slots, energies, contour,
    )


def solution(mesh):
    return jax.shard_map(
        body,
        mesh=mesh,
        in_specs=(
            P("chan", None, None),
            P("mult", None, "chan", None),
            P("chan", None, "mult"),
            P("chan", None),
            P("chan"),
            P("chan", None),
            P("chan", None),
            P("chan"),
            P(),
        ),
        out_specs=P("chan", "mult", None),
        check_vma=False,
    )
```

```python
import jax
import jax.numpy as jnp
from jax import lax
from jax.experimental import pallas as pl
from jax.experimental.pallas import tpu as pltpu
from jax.sharding import PartitionSpec as P

MAXNZ = 16
MESH = pl.DeviceIdType.MESH
F32 = jnp.float32
BF16 = jnp.bfloat16
NB = 1024


def device(z_lo, core, z_hi, x, y):
    return (z_lo * 2 + core, z_hi * 16 + x * 4 + y)


def split(value):
    high = value.astype(BF16)
    return high, (value - high.astype(F32)).astype(BF16)


def swap_halves(value):
    lane = lax.broadcasted_iota(jnp.int32, value.shape, value.ndim - 1)
    rolled = pltpu.roll(value, 64, value.ndim - 1)
    return jnp.where(lane < 64, -rolled, rolled)


def own_mixing(coefficients, channel_cols, lambda_low, lambda_high, used_slots, mine):
    mi = lax.axis_index("mult")
    ci = lax.axis_index("chan")
    lane = lax.broadcasted_iota(jnp.int32, (8, 128), 1)
    row = lax.broadcasted_iota(jnp.int32, (8, 128), 0)
    order = lane % 8
    used = jnp.zeros((8, 128), jnp.int32)
    for i in range(8):
        used = jnp.where(row == i, used_slots[i], used)
    own_order = (order // 2 == mi) & (lane < 64)

    def wide(ref_value, s):
        return jnp.broadcast_to(ref_value[:, s:s + 1], (8, 128))

    even, odd = coefficients[0], coefficients[1]
    low, high, cols = lambda_low[...], lambda_high[...], channel_cols[...]
    sums = [jnp.zeros((8, 128), F32) for _ in range(5)]
    for s in range(MAXNZ):
        value = jnp.where(order % 2 == 0, wide(even, s), wide(odd, s))
        keep = own_order & (used > s) & (order >= wide(low, s)) & (order < wide(high, s))
        value = jnp.where(keep, value, 0.0)
        local = wide(cols, s) - (ci - 2) * 8 - lane // 8
        for d in range(5):
            sums[d] += jnp.where(local == d * 8, value, 0.0)
    mine[...] = jnp.concatenate(sums, axis=0)


def kernel(
    columns, panels, coefficients, channel_cols, lambda_low, lambda_high, used_slots, energies, contour, out,
    raw, p_high, p_low, blocks, x_high, x_low, z_first, z_second,
    mine, parts, mix_rows, mix_high, mix_low, coupled, near, far,
    own_sem, first_send, p_send, p_recv, x_send, f_send, z_send, x_recv, s_send, s_recv,
    part_send, part_recv, row_send, row_recv, pair_send, pair_recv, near_send, near_sem, far_send, far_sem,
):
    mi = lax.axis_index("mult")
    ci = lax.axis_index("chan")
    z_lo, core, z_hi, x, y = mi // 2, mi % 2, ci // 16, (ci // 4) % 4, ci % 4
    left_x, right_x = (x + 3) % 4, (x + 1) % 4
    left_y, right_y = (y + 3) % 4, (y + 1) % 4
    to_left_x = device(z_lo, core, z_hi, left_x, y)
    to_right_x = device(z_lo, core, z_hi, right_x, y)
    to_left_y = device(z_lo, core, z_hi, x, left_y)
    to_right_y = device(z_lo, core, z_hi, x, right_y)
    sibling = device(z_lo, 1 - core, z_hi, x, y)
    partner = device(1 - z_lo, core, z_hi, x, y)
    full = z_lo == core
    target_x = (x + 2 * core + 3) % 4
    targets = [device(z_hi, x // 2, zh, target_x, y) for zh in range(2)]

    def origin(at_x):
        row_part = 1 - at_x % 2
        from_x = 2 * core + row_part
        from_core = jnp.where((from_x + 1) % 4 == at_x, 1, 0)
        return row_part, from_x, from_core

    _, from_x0, from_core0 = origin(x)
    sources = [device(zl, from_core0, z_lo, from_x0, y) for zl in range(2)]
    spots = [origin(at) for at in (x, left_x, right_x, (x + 2) % 4)]
    first_part, second_part = x % 2, 1 - x % 2

    group = ci // 4
    below = (mi, (group + 7) % 8 * 4 + y)
    above = (mi, (group + 1) % 8 * 4 + y)
    mates = [(mi, group * 4 + (y + k) % 4) for k in range(1, 4)]
    others = [((mi + k) % 4, ci) for k in range(1, 4)]

    barrier = pltpu.get_barrier_semaphore()
    peers = [to_left_x, to_right_x, below, above] + targets + sources + others + mates
    for peer in peers:
        pl.semaphore_signal(barrier, inc=1, device_id=peer, device_id_type=MESH)

    own = pltpu.make_async_copy(columns, blocks.at[0], own_sem)
    own.start()
    own_mixing(coefficients, channel_cols, lambda_low, lambda_high, used_slots, mine)
    coupled[...] = jnp.zeros_like(coupled)
    pl.semaphore_wait(barrier, len(peers))

    def remote(src, dst, send_sem, recv_sem, peer):
        return pltpu.make_async_remote_copy(
            src_ref=src, dst_ref=dst, send_sem=send_sem, recv_sem=recv_sem,
            device_id=peer, device_id_type=MESH,
        )

    sent = []
    sent_full = []

    def start(copy):
        copy.start()
        sent.append(copy)

    for k in range(3):
        start(remote(mine, parts.at[2 - k], part_send.at[k], part_recv.at[2 - k], others[k]))

    for k in range(2):
        start(remote(panels, raw.at[0, z_lo], first_send.at[k], p_recv.at[0, z_lo], targets[k]))

    for k in range(3):
        remote(mine, parts.at[k], part_send.at[k], part_recv.at[k], others[k]).wait_recv()
    mix_rows[y + 2] = mine[...] + parts[0] + parts[1] + parts[2]
    for k in range(3):
        start(remote(mix_rows.at[y + 2], mix_rows.at[y + 2], row_send.at[k], row_recv.at[y], mates[k]))

    def channel(e, s):
        return 4 * core + 2 * e + s

    def own_copies(e):
        copies = []
        for s_right, s_left in ((0, 1), (1, 0)):
            c_right, c_left = channel(e, s_right), channel(e, s_left)
            copies.append(remote(columns.at[c_right], blocks.at[1, c_right],
                                 x_send.at[0, e, s_right], x_recv.at[1, e, s_right], to_right_y))
            copies.append(remote(columns.at[c_left], blocks.at[2, c_left],
                                 x_send.at[1, e, s_left], x_recv.at[2, e, s_left], to_left_y))
        return copies

    common, extra = own_copies(0), own_copies(1)

    @pl.when(full)
    def _():
        for copy in extra[:2]:
            copy.start()

    for copy in common[:2]:
        start(copy)

    @pl.when(full)
    def _():
        for copy in extra[2:]:
            copy.start()

    for copy in common[2:]:
        start(copy)
    sent_full += extra
    for k in range(1, 4):
        ref = mix_rows.at[2 + (y + k) % 4]
        remote(ref, ref, row_send.at[0], row_recv.at[(y + k) % 4], mates[0]).wait_recv()
    start(remote(mix_rows.at[pl.ds(2, 2)], mix_rows.at[pl.ds(6, 2)], pair_send.at[0], pair_recv.at[0], below))
    start(remote(mix_rows.at[pl.ds(4, 2)], mix_rows.at[pl.ds(0, 2)], pair_send.at[1], pair_recv.at[1], above))

    def wait_p(slot, zl):
        ref = raw.at[slot, zl]
        remote(ref, ref, p_send.at[0, zl], p_recv.at[slot, zl], to_right_x).wait_recv()

    def forward_p(zl):
        slot, peer = (1, to_right_x) if zl == 0 else (2, to_left_x)
        start(remote(raw.at[slot, zl], raw.at[3, zl], p_send.at[2, zl], p_recv.at[3, zl], peer))

    def wait_x(b, e, s):
        ref = blocks.at[b, channel(e, s)]
        remote(ref, ref, x_send.at[0, e, s], x_recv.at[b, e, s], to_right_y).wait_recv()

    def forward_x(e, s):
        c = channel(e, s)
        b, peer = (1, to_right_y) if s == 0 else (2, to_left_y)
        return remote(blocks.at[b, c], blocks.at[3, c], f_send.at[e, s], x_recv.at[3, e, s], peer)

    def to_partner(b, s):
        ref = blocks.at[b, channel(1, s)]
        return remote(ref, ref, z_send.at[b, s], x_recv.at[b, 1, s], partner)

    def to_sibling(b, e, s):
        ref = blocks.at[b, channel(e, s)]
        start(remote(ref, ref, s_send.at[b, e, s], s_recv.at[b, e, s], sibling))

    def wait_sibling(b):
        for e in range(2):
            for s in range(2):
                ref = blocks.at[b, 4 * (1 - core) + 2 * e + s]
                remote(ref, ref, s_send.at[b, e, s], s_recv.at[b, e, s], sibling).wait_recv()

    def take_extra(pairs, onward):
        @pl.when(full)
        def _():
            for b, s in pairs:
                wait_x(b, 1, s)
                if onward:
                    forward_x(1, s).start()
                to_partner(b, s).start()

        for b, s in pairs:
            if onward:
                sent_full.append(forward_x(1, s))
            sent_full.append(to_partner(b, s))

    def pass_extra(pairs):
        @pl.when(jnp.logical_not(full))
        def _():
            for b, s in pairs:
                wait_x(b, 1, s)

        for b, s in pairs:
            to_sibling(b, 1, s)

    def convert_p(slot):
        row_part, _, from_core = spots[slot]
        for zl in range(2):
            for order in range(2):
                at = row_part * 8 + 4 * zl + 2 * from_core + order
                for ri in range(2):
                    high, low = split(raw[slot, zl, order, ri])
                    p_high[at, ri] = high
                    p_low[at, ri] = low

    def half(k):
        return (core + k) % 2

    def convert_x(b, k):
        h = half(k)
        for quarter in range(4):
            high, low = split(blocks[b, 4 * h + quarter])
            x_high[b, h, :, quarter * 128:quarter * 128 + 128] = high
            x_low[b, h, :, quarter * 128:quarter * 128 + 128] = low

    def multiply(ph, plo, b, h):
        acc = jnp.dot(ph, x_high[b, h], preferred_element_type=F32)
        acc += jnp.dot(plo, x_high[b, h], preferred_element_type=F32)
        acc += jnp.dot(ph, x_low[b, h], preferred_element_type=F32)
        return acc

    def store(ref, acc, count, at, chan):
        acc = acc.reshape(count, 2, 32, 512)
        for quarter in range(4):
            part = acc[..., quarter * 128:quarter * 128 + 128]
            ref[chan + quarter, pl.ds(at, count)] = part[:, 0] + swap_halves(part[:, 1])

    def each(run, halves):
        def step(k, carry):
            run(half(k))
            return carry

        lax.fori_loop(halves[0], halves[-1] + 1, step, 0)

    def unit_slot(slot, b, halves=(0, 1)):
        row_part, _, from_core = spots[slot]
        ats = [4 * zl + 2 * from_core for zl in range(2)]

        def run(h):
            ph = jnp.concatenate([p_high[pl.ds(row_part * 8 + at, 2)] for at in ats], axis=0)
            plo = jnp.concatenate([p_low[pl.ds(row_part * 8 + at, 2)] for at in ats], axis=0)
            acc = multiply(ph.reshape(256, NB), plo.reshape(256, NB), b, h)
            for zl in range(2):
                store(z_second, acc[zl * 128:zl * 128 + 128], 2, ats[zl], b * 8 + 4 * h)

        each(run, halves)

    def unit_part(part, ref, base, b, halves=(0, 1)):
        def run(h):
            ph = p_high[pl.ds(part * 8, 8)].reshape(512, NB)
            plo = p_low[pl.ds(part * 8, 8)].reshape(512, NB)
            store(ref, multiply(ph, plo, b, h), 8, 0, base + 4 * h)

        each(run, halves)

    def unit_first(b, halves=(0, 1)):
        unit_part(first_part, z_first, 8 * (b == 2), b, halves)

    def mix_first(b):
        mix(z_first, 8 * (b == 2), b, first_part)

    def mix_second(b):
        mix(z_second, b * 8, b, second_part)

    at_y = [y, left_y, right_y, (y + 2) % 4]

    def mix(ref, base, b, part):
        t = at_y[b]

        def step(k, carry):
            first = pl.multiple_of(k * 16, 16)
            tile = ref[pl.ds(base, 8), :, pl.ds(first, 16), :]
            both = jnp.concatenate(
                [tile[:, :, :8].reshape(512, 128), tile[:, :, 8:].reshape(512, 128)], axis=1
            )
            high, low = split(both)
            acc = jnp.dot(mix_high[t], high, preferred_element_type=F32)
            acc += jnp.dot(mix_high[t], low, preferred_element_type=F32)
            acc += jnp.dot(mix_low[t], high, preferred_element_type=F32)
            for half in range(2):
                new = acc[:, half * 128:half * 128 + 128].reshape(5, 8, 8, 128)
                at = pl.multiple_of(first + half * 8, 8)
                coupled[part, pl.ds(t, 5), :, pl.ds(at, 8), :] += new
            return carry

        lax.fori_loop(0, 2, step, 0)

    def far_copies(part):
        return [
            remote(coupled.at[part, pl.ds(0, 2)], far.at[part, 1], far_send.at[part, 0], far_sem.at[part, 1], below),
            remote(coupled.at[part, pl.ds(6, 2)], far.at[part, 0], far_send.at[part, 1], far_sem.at[part, 0], above),
        ]

    def near_copies(part):
        return [
            remote(coupled.at[part, 2 + (y + k) % 4], near.at[part, y], near_send.at[part, k - 1],
                   near_sem.at[part, y], mates[k - 1])
            for k in range(1, 4)
        ]

    def send_far(part):
        for copy in far_copies(part):
            start(copy)

    def send_near(part):
        for k in range(2):
            ref = far.at[part, k]
            remote(ref, ref, far_send.at[part, k], far_sem.at[part, k], below).wait_recv()
            coupled[part, pl.ds(2 + 2 * k, 2)] += far[part, k]
        for copy in near_copies(part):
            start(copy)
        near[part, y] = coupled[part, 2 + y]

    def finish(part):
        for k in range(1, 4):
            ref = near.at[part, (y + k) % 4]
            remote(ref, ref, near_send.at[part, 0], near_sem.at[part, (y + k) % 4], mates[0]).wait_recv()
        lane = lax.broadcasted_iota(jnp.int32, (32, 128), 1)
        turn = jnp.where(lane < 64, -contour[1], contour[1])
        for k in range(4):
            at = part * 128 + k * 32
            for i in range(8):
                cols = blocks[0, i, pl.ds(pl.multiple_of(mi * 256 + at, 32), 32), :]
                out[i, pl.ds(pl.multiple_of(at, 32), 32), :] = (
                    (contour[0] - energies[i]) * cols + turn * pltpu.roll(cols, 64, 1) - near[part, k, i]
                )

    def build_mix():
        wide_row = lax.broadcasted_iota(jnp.int32, (128, 512), 0)
        wide_lane = lax.broadcasted_iota(jnp.int32, (128, 512), 1)
        widen = jnp.where(wide_lane // 8 == wide_row, 1.0, 0.0).astype(BF16)
        lane = lax.broadcasted_iota(jnp.int32, (320, 512), 1)
        row = lax.broadcasted_iota(jnp.int32, (320, 512), 0)
        same = (lane % 8) == (row % 8)
        for t in range(4):
            rows = jnp.concatenate([mix_rows[t + k, 8 * (4 - k):8 * (4 - k) + 8] for k in range(5)], axis=0)
            for ref, value in zip((mix_high, mix_low), split(rows)):
                wide = jnp.dot(value, widen, preferred_element_type=F32)
                wide = jnp.broadcast_to(wide[:, None, :], (40, 8, 512)).reshape(320, 512)
                ref[t] = jnp.where(same, wide, 0.0).astype(BF16)

    own.wait()
    for k in range(2):
        convert_x(0, k)

    for zl in range(2):
        wait_p(0, zl)
    for zl_right, zl_left in ((0, 1), (1, 0)):
        start(remote(raw.at[0, zl_right], raw.at[1, zl_right], p_send.at[0, zl_right],
                     p_recv.at[1, zl_right], to_right_x))
        start(remote(raw.at[0, zl_left], raw.at[2, zl_left], p_send.at[1, zl_left],
                     p_recv.at[2, zl_left], to_left_x))
    convert_p(0)
    unit_slot(0, 0)

    early, late, last = ((1, 0), (2, 1)), ((1, 1), (2, 0)), ((3, 0), (3, 1))
    take_extra(early, True)
    for b, s in early:
        wait_x(b, 0, s)
        start(forward_x(0, s))
        to_sibling(b, 0, s)
    for zl in range(2):
        wait_p(1 + zl, zl)
        forward_p(zl)
    for k in range(2):
        ref = mix_rows.at[pl.ds(6 - 6 * k, 2)]
        remote(ref, ref, pair_send.at[k], pair_recv.at[k], below).wait_recv()
    build_mix()
    take_extra(late, False)
    for b, s in late:
        wait_x(b, 0, s)
        to_sibling(b, 0, s)
    wait_p(1, 1)
    convert_p(1)
    wait_p(2, 0)
    convert_p(2)
    unit_first(0)
    pass_extra(early)
    pass_extra(late)
    mix_first(0)
    for b in (1, 2):
        convert_x(b, 0)
        unit_slot(0, b, (0,))
    unit_first(1, (0,))
    take_extra(last, False)
    for b, s in last:
        wait_x(b, 0, s)
        to_sibling(b, 0, s)
    unit_first(2, (0,))
    wait_sibling(1)
    convert_x(1, 1)
    unit_slot(0, 1, (1,))
    unit_first(1, (1,))
    pass_extra(last)
    mix_first(1)
    wait_sibling(2)
    convert_x(2, 1)
    unit_slot(0, 2, (1,))
    unit_first(2, (1,))
    mix_first(2)
    convert_x(3, 0)
    wait_sibling(3)
    convert_x(3, 1)
    unit_first(3)
    mix_first(3)
    send_far(first_part)
    wait_p(3, 0)
    wait_p(3, 1)
    convert_p(3)
    for b in range(3):
        unit_slot(3, b)
        mix_second(b)
    unit_part(second_part, z_second, 24, 3)
    mix_second(3)
    send_far(second_part)
    send_near(second_part)
    send_near(first_part)
    finish(second_part)
    finish(first_part)

    for copy in sent:
        copy.wait_send()

    @pl.when(full)
    def _():
        for copy in sent_full:
            copy.wait_send()


def filter_step(*operands):
    dma = pltpu.SemaphoreType.DMA
    vmem = pl.BlockSpec(memory_space=pltpu.VMEM)
    smem = pl.BlockSpec(memory_space=pltpu.SMEM)
    anywhere = pl.BlockSpec(memory_space=pl.ANY)
    return pl.pallas_call(
        kernel,
        out_shape=jax.ShapeDtypeStruct((8, 256, 128), F32),
        in_specs=[anywhere] * 2 + [vmem] * 4 + [smem] * 3,
        out_specs=vmem,
        scratch_shapes=[
            pltpu.VMEM((4, 2, 2, 2, 32, NB), F32),
            pltpu.VMEM((16, 2, 32, NB), BF16),
            pltpu.VMEM((16, 2, 32, NB), BF16),
            pltpu.VMEM((4, 8, NB, 128), F32),
            pltpu.VMEM((4, 2, NB, 512), BF16),
            pltpu.VMEM((4, 2, NB, 512), BF16),
            pltpu.VMEM((16, 8, 32, 128), F32),
            pltpu.VMEM((32, 8, 32, 128), F32),
            pltpu.VMEM((40, 128), F32),
            pltpu.VMEM((3, 40, 128), F32),
            pltpu.VMEM((8, 40, 128), F32),
            pltpu.VMEM((4, 320, 512), BF16),
            pltpu.VMEM((4, 320, 512), BF16),
            pltpu.VMEM((2, 8, 8, 32, 128), F32),
            pltpu.VMEM((2, 4, 8, 32, 128), F32),
            pltpu.VMEM((2, 2, 2, 8, 32, 128), F32),
            dma, dma((2,)), dma((3, 2)), dma((4, 2)),
            dma((2, 2, 2)), dma((2, 2)), dma((4, 2)), dma((4, 2, 2)), dma((4, 2, 2)), dma((4, 2, 2)),
            dma((3,)), dma((3,)), dma((3,)), dma((4,)), dma((2,)), dma((2,)),
            dma((2, 3)), dma((2, 4)), dma((2, 2)), dma((2, 2)),
        ],
        compiler_params=pltpu.CompilerParams(
            collective_id=0, has_side_effects=True, vmem_limit_bytes=60 * 2**20
        ),
        cost_estimate=pl.CostEstimate(flops=30_000_000_000, bytes_accessed=40_000_000, transcendentals=0),
        name="filter_step",
    )(*operands)


def body(
    columns, panels, coefficients, channel_cols, used_slots, lambda_low, lambda_high, energies, contour
):
    return filter_step(
        columns, panels, jnp.transpose(coefficients, (2, 0, 1)), channel_cols, lambda_low, lambda_high,
        used_slots, energies, contour,
    )


def solution(mesh):
    return jax.shard_map(
        body,
        mesh=mesh,
        in_specs=(
            P("chan", None, None),
            P("mult", None, "chan", None),
            P("chan", None, "mult"),
            P("chan", None),
            P("chan"),
            P("chan", None),
            P("chan", None),
            P("chan"),
            P(),
        ),
        out_specs=P("chan", "mult", None),
        check_vma=False,
    )
```

```python
import jax
import jax.numpy as jnp
from jax import lax
from jax.experimental import pallas as pl
from jax.experimental.pallas import tpu as pltpu
from jax.sharding import PartitionSpec as P

MAXNZ = 16
MESH = pl.DeviceIdType.MESH
F32 = jnp.float32
BF16 = jnp.bfloat16
NB = 1024


def device(z_lo, core, z_hi, x, y):
    return (z_lo * 2 + core, z_hi * 16 + x * 4 + y)


def split(value):
    high = value.astype(BF16)
    return high, (value - high.astype(F32)).astype(BF16)


def swap_halves(value):
    lane = lax.broadcasted_iota(jnp.int32, value.shape, value.ndim - 1)
    rolled = pltpu.roll(value, 64, value.ndim - 1)
    return jnp.where(lane < 64, -rolled, rolled)


def own_mixing(coefficients, channel_cols, lambda_low, lambda_high, used_slots, mine):
    mi = lax.axis_index("mult")
    ci = lax.axis_index("chan")
    lane = lax.broadcasted_iota(jnp.int32, (8, 128), 1)
    row = lax.broadcasted_iota(jnp.int32, (8, 128), 0)
    order = lane % 8
    used = jnp.zeros((8, 128), jnp.int32)
    for i in range(8):
        used = jnp.where(row == i, used_slots[i], used)
    own_order = (order // 2 == mi) & (lane < 64)

    def wide(ref_value, s):
        return jnp.broadcast_to(ref_value[:, s:s + 1], (8, 128))

    even, odd = coefficients[0], coefficients[1]
    low, high, cols = lambda_low[...], lambda_high[...], channel_cols[...]
    sums = [jnp.zeros((8, 128), F32) for _ in range(5)]
    for s in range(MAXNZ):
        value = jnp.where(order % 2 == 0, wide(even, s), wide(odd, s))
        keep = own_order & (used > s) & (order >= wide(low, s)) & (order < wide(high, s))
        value = jnp.where(keep, value, 0.0)
        local = wide(cols, s) - (ci - 2) * 8 - lane // 8
        for d in range(5):
            sums[d] += jnp.where(local == d * 8, value, 0.0)
    mine[...] = jnp.concatenate(sums, axis=0)


def kernel(
    columns, panels, coefficients, channel_cols, lambda_low, lambda_high, used_slots, energies, contour, out,
    raw, p_high, p_low, blocks, x_high, x_low, z_first, z_second,
    mine, parts, mix_rows, mix_high, mix_low, coupled, near, far,
    own_sem, first_send, p_send, p_recv, x_send, f_send, z_send, x_recv, s_send, s_recv,
    part_send, part_recv, row_send, row_recv, pair_send, pair_recv, near_send, near_sem, far_send, far_sem,
):
    mi = lax.axis_index("mult")
    ci = lax.axis_index("chan")
    z_lo, core, z_hi, x, y = mi // 2, mi % 2, ci // 16, (ci // 4) % 4, ci % 4
    left_x, right_x = (x + 3) % 4, (x + 1) % 4
    left_y, right_y = (y + 3) % 4, (y + 1) % 4
    to_left_x = device(z_lo, core, z_hi, left_x, y)
    to_right_x = device(z_lo, core, z_hi, right_x, y)
    to_left_y = device(z_lo, core, z_hi, x, left_y)
    to_right_y = device(z_lo, core, z_hi, x, right_y)
    sibling = device(z_lo, 1 - core, z_hi, x, y)
    partner = device(1 - z_lo, core, z_hi, x, y)
    full = z_lo == core
    target_x = (x + 2 * core + 3) % 4
    targets = [device(z_hi, x // 2, zh, target_x, y) for zh in range(2)]

    def origin(at_x):
        row_part = 1 - at_x % 2
        from_x = 2 * core + row_part
        from_core = jnp.where((from_x + 1) % 4 == at_x, 1, 0)
        return row_part, from_x, from_core

    _, from_x0, from_core0 = origin(x)
    sources = [device(zl, from_core0, z_lo, from_x0, y) for zl in range(2)]
    spots = [origin(at) for at in (x, left_x, right_x, (x + 2) % 4)]
    first_part, second_part = x % 2, 1 - x % 2

    group = ci // 4
    below = (mi, (group + 7) % 8 * 4 + y)
    above = (mi, (group + 1) % 8 * 4 + y)
    mates = [(mi, group * 4 + (y + k) % 4) for k in range(1, 4)]
    others = [((mi + k) % 4, ci) for k in range(1, 4)]

    barrier = pltpu.get_barrier_semaphore()
    peers = [to_left_x, to_right_x, below, above] + targets + sources + others + mates
    for peer in peers:
        pl.semaphore_signal(barrier, inc=1, device_id=peer, device_id_type=MESH)

    own = pltpu.make_async_copy(columns, blocks.at[0], own_sem)
    own.start()
    own_mixing(coefficients, channel_cols, lambda_low, lambda_high, used_slots, mine)
    coupled[...] = jnp.zeros_like(coupled)
    pl.semaphore_wait(barrier, len(peers))

    def remote(src, dst, send_sem, recv_sem, peer):
        return pltpu.make_async_remote_copy(
            src_ref=src, dst_ref=dst, send_sem=send_sem, recv_sem=recv_sem,
            device_id=peer, device_id_type=MESH,
        )

    sent = []
    sent_full = []

    def start(copy):
        copy.start()
        sent.append(copy)

    for k in range(3):
        start(remote(mine, parts.at[2 - k], part_send.at[k], part_recv.at[2 - k], others[k]))

    for k in range(2):
        start(remote(panels, raw.at[0, z_lo], first_send.at[k], p_recv.at[0, z_lo], targets[k]))

    for k in range(3):
        remote(mine, parts.at[k], part_send.at[k], part_recv.at[k], others[k]).wait_recv()
    mix_rows[y + 2] = mine[...] + parts[0] + parts[1] + parts[2]
    for k in range(3):
        start(remote(mix_rows.at[y + 2], mix_rows.at[y + 2], row_send.at[k], row_recv.at[y], mates[k]))

    def channel(e, s):
        return 4 * core + 2 * e + s

    def own_copies(e):
        copies = []
        for s_right, s_left in ((0, 1), (1, 0)):
            c_right, c_left = channel(e, s_right), channel(e, s_left)
            copies.append(remote(columns.at[c_right], blocks.at[1, c_right],
                                 x_send.at[0, e, s_right], x_recv.at[1, e, s_right], to_right_y))
            copies.append(remote(columns.at[c_left], blocks.at[2, c_left],
                                 x_send.at[1, e, s_left], x_recv.at[2, e, s_left], to_left_y))
        return copies

    common, extra = own_copies(0), own_copies(1)

    @pl.when(full)
    def _():
        for copy in extra[:2]:
            copy.start()

    for copy in common[:2]:
        start(copy)

    @pl.when(full)
    def _():
        for copy in extra[2:]:
            copy.start()

    for copy in common[2:]:
        start(copy)
    sent_full += extra
    for k in range(1, 4):
        ref = mix_rows.at[2 + (y + k) % 4]
        remote(ref, ref, row_send.at[0], row_recv.at[(y + k) % 4], mates[0]).wait_recv()
    start(remote(mix_rows.at[pl.ds(2, 2)], mix_rows.at[pl.ds(6, 2)], pair_send.at[0], pair_recv.at[0], below))
    start(remote(mix_rows.at[pl.ds(4, 2)], mix_rows.at[pl.ds(0, 2)], pair_send.at[1], pair_recv.at[1], above))

    def wait_p(slot, zl):
        ref = raw.at[slot, zl]
        remote(ref, ref, p_send.at[0, zl], p_recv.at[slot, zl], to_right_x).wait_recv()

    def forward_p(zl):
        slot, peer = (1, to_right_x) if zl == 0 else (2, to_left_x)
        start(remote(raw.at[slot, zl], raw.at[3, zl], p_send.at[2, zl], p_recv.at[3, zl], peer))

    def wait_x(b, e, s):
        ref = blocks.at[b, channel(e, s)]
        remote(ref, ref, x_send.at[0, e, s], x_recv.at[b, e, s], to_right_y).wait_recv()

    def forward_x(e, s):
        c = channel(e, s)
        b, peer = (1, to_right_y) if s == 0 else (2, to_left_y)
        return remote(blocks.at[b, c], blocks.at[3, c], f_send.at[e, s], x_recv.at[3, e, s], peer)

    def to_partner(b, s):
        ref = blocks.at[b, channel(1, s)]
        return remote(ref, ref, z_send.at[b, s], x_recv.at[b, 1, s], partner)

    def to_sibling(b, e, s):
        ref = blocks.at[b, channel(e, s)]
        start(remote(ref, ref, s_send.at[b, e, s], s_recv.at[b, e, s], sibling))

    def wait_sibling(b):
        for e in range(2):
            for s in range(2):
                ref = blocks.at[b, 4 * (1 - core) + 2 * e + s]
                remote(ref, ref, s_send.at[b, e, s], s_recv.at[b, e, s], sibling).wait_recv()

    def take_extra(pairs, onward):
        @pl.when(full)
        def _():
            for b, s in pairs:
                wait_x(b, 1, s)
                if onward:
                    forward_x(1, s).start()
                to_partner(b, s).start()

        for b, s in pairs:
            if onward:
                sent_full.append(forward_x(1, s))
            sent_full.append(to_partner(b, s))

    def pass_extra(pairs):
        @pl.when(jnp.logical_not(full))
        def _():
            for b, s in pairs:
                wait_x(b, 1, s)

        for b, s in pairs:
            to_sibling(b, 1, s)

    def convert_p(slot):
        row_part, _, from_core = spots[slot]
        for zl in range(2):
            for order in range(2):
                at = row_part * 8 + 4 * zl + 2 * from_core + order
                for ri in range(2):
                    high, low = split(raw[slot, zl, order, ri])
                    p_high[at, ri] = high
                    p_low[at, ri] = low

    def half(k):
        return (core + k) % 2

    def convert_x(b, k):
        h = half(k)
        for quarter in range(4):
            high, low = split(blocks[b, 4 * h + quarter])
            x_high[b, h, :, quarter * 128:quarter * 128 + 128] = high
            x_low[b, h, :, quarter * 128:quarter * 128 + 128] = low

    def multiply(ph, plo, b, h):
        acc = jnp.dot(ph, x_high[b, h], preferred_element_type=F32)
        acc += jnp.dot(plo, x_high[b, h], preferred_element_type=F32)
        acc += jnp.dot(ph, x_low[b, h], preferred_element_type=F32)
        return acc

    def store(ref, acc, count, at, chan):
        acc = acc.reshape(count, 2, 32, 512)
        for quarter in range(4):
            part = acc[..., quarter * 128:quarter * 128 + 128]
            ref[chan + quarter, pl.ds(at, count)] = part[:, 0] + swap_halves(part[:, 1])

    def each(run, halves):
        def step(k, carry):
            run(half(k))
            return carry

        lax.fori_loop(halves[0], halves[-1] + 1, step, 0)

    def unit_slot(slot, b, halves=(0, 1)):
        row_part, _, from_core = spots[slot]
        ats = [4 * zl + 2 * from_core for zl in range(2)]

        def run(h):
            ph = jnp.concatenate([p_high[pl.ds(row_part * 8 + at, 2)] for at in ats], axis=0)
            plo = jnp.concatenate([p_low[pl.ds(row_part * 8 + at, 2)] for at in ats], axis=0)
            acc = multiply(ph.reshape(256, NB), plo.reshape(256, NB), b, h)
            for zl in range(2):
                store(z_second, acc[zl * 128:zl * 128 + 128], 2, ats[zl], b * 8 + 4 * h)

        each(run, halves)

    def unit_part(part, ref, base, b, halves=(0, 1)):
        def run(h):
            ph = p_high[pl.ds(part * 8, 8)].reshape(512, NB)
            plo = p_low[pl.ds(part * 8, 8)].reshape(512, NB)
            store(ref, multiply(ph, plo, b, h), 8, 0, base + 4 * h)

        each(run, halves)

    def unit_first(b, halves=(0, 1)):
        unit_part(first_part, z_first, 8 * (b == 2), b, halves)

    def mix_first(b):
        mix(z_first, 8 * (b == 2), b, first_part)

    def mix_second(b):
        mix(z_second, b * 8, b, second_part)

    at_y = [y, left_y, right_y, (y + 2) % 4]

    def mix(ref, base, b, part):
        t = at_y[b]

        def step(k, carry):
            first = pl.multiple_of(k * 16, 16)
            tile = ref[pl.ds(base, 8), :, pl.ds(first, 16), :]
            both = jnp.concatenate(
                [tile[:, :, :8].reshape(512, 128), tile[:, :, 8:].reshape(512, 128)], axis=1
            )
            high, low = split(both)
            acc = jnp.dot(mix_high[t], high, preferred_element_type=F32)
            acc += jnp.dot(mix_high[t], low, preferred_element_type=F32)
            acc += jnp.dot(mix_low[t], high, preferred_element_type=F32)
            for half in range(2):
                new = acc[:, half * 128:half * 128 + 128].reshape(5, 8, 8, 128)
                at = pl.multiple_of(first + half * 8, 8)
                coupled[part, pl.ds(t, 5), :, pl.ds(at, 8), :] += new
            return carry

        lax.fori_loop(0, 2, step, 0)

    def far_copies(part):
        return [
            remote(coupled.at[part, pl.ds(0, 2)], far.at[part, 1], far_send.at[part, 0], far_sem.at[part, 1], below),
            remote(coupled.at[part, pl.ds(6, 2)], far.at[part, 0], far_send.at[part, 1], far_sem.at[part, 0], above),
        ]

    def near_copies(part):
        return [
            remote(coupled.at[part, 2 + (y + k) % 4], near.at[part, y], near_send.at[part, k - 1],
                   near_sem.at[part, y], mates[k - 1])
            for k in range(1, 4)
        ]

    def send_far(part):
        for copy in far_copies(part):
            start(copy)

    def send_near(part):
        for k in range(2):
            ref = far.at[part, k]
            remote(ref, ref, far_send.at[part, k], far_sem.at[part, k], below).wait_recv()
            coupled[part, pl.ds(2 + 2 * k, 2)] += far[part, k]
        for copy in near_copies(part):
            start(copy)
        near[part, y] = coupled[part, 2 + y]

    def finish(part):
        for k in range(1, 4):
            ref = near.at[part, (y + k) % 4]
            remote(ref, ref, near_send.at[part, 0], near_sem.at[part, (y + k) % 4], mates[0]).wait_recv()
        lane = lax.broadcasted_iota(jnp.int32, (32, 128), 1)
        turn = jnp.where(lane < 64, -contour[1], contour[1])
        for k in range(4):
            at = part * 128 + k * 32
            for i in range(8):
                cols = blocks[0, i, pl.ds(pl.multiple_of(mi * 256 + at, 32), 32), :]
                out[i, pl.ds(pl.multiple_of(at, 32), 32), :] = (
                    (contour[0] - energies[i]) * cols + turn * pltpu.roll(cols, 64, 1) - near[part, k, i]
                )

    def build_mix():
        wide_row = lax.broadcasted_iota(jnp.int32, (128, 512), 0)
        wide_lane = lax.broadcasted_iota(jnp.int32, (128, 512), 1)
        widen = jnp.where(wide_lane // 8 == wide_row, 1.0, 0.0).astype(BF16)
        lane = lax.broadcasted_iota(jnp.int32, (320, 512), 1)
        row = lax.broadcasted_iota(jnp.int32, (320, 512), 0)
        same = (lane % 8) == (row % 8)
        for t in range(4):
            rows = jnp.concatenate([mix_rows[t + k, 8 * (4 - k):8 * (4 - k) + 8] for k in range(5)], axis=0)
            for ref, value in zip((mix_high, mix_low), split(rows)):
                wide = jnp.dot(value, widen, preferred_element_type=F32)
                wide = jnp.broadcast_to(wide[:, None, :], (40, 8, 512)).reshape(320, 512)
                ref[t] = jnp.where(same, wide, 0.0).astype(BF16)

    own.wait()
    for k in range(2):
        convert_x(0, k)

    for zl in range(2):
        wait_p(0, zl)
    for zl_right, zl_left in ((0, 1), (1, 0)):
        start(remote(raw.at[0, zl_right], raw.at[1, zl_right], p_send.at[0, zl_right],
                     p_recv.at[1, zl_right], to_right_x))
        start(remote(raw.at[0, zl_left], raw.at[2, zl_left], p_send.at[1, zl_left],
                     p_recv.at[2, zl_left], to_left_x))
    convert_p(0)
    unit_slot(0, 0)

    early, late, last = ((1, 0), (2, 1)), ((1, 1), (2, 0)), ((3, 0), (3, 1))
    take_extra(early, True)
    for b, s in early:
        wait_x(b, 0, s)
        start(forward_x(0, s))
        to_sibling(b, 0, s)
    for zl in range(2):
        wait_p(1 + zl, zl)
        forward_p(zl)
    for k in range(2):
        ref = mix_rows.at[pl.ds(6 - 6 * k, 2)]
        remote(ref, ref, pair_send.at[k], pair_recv.at[k], below).wait_recv()
    build_mix()
    take_extra(late, False)
    for b, s in late:
        wait_x(b, 0, s)
        to_sibling(b, 0, s)
    wait_p(1, 1)
    convert_p(1)
    wait_p(2, 0)
    convert_p(2)
    unit_first(0)
    pass_extra(early)
    pass_extra(late)
    mix_first(0)
    for b in (1, 2):
        convert_x(b, 0)
        unit_slot(0, b, (0,))
    take_extra(last, False)
    for b, s in last:
        wait_x(b, 0, s)
        to_sibling(b, 0, s)
    unit_first(1, (0,))
    unit_first(2, (0,))
    wait_sibling(1)
    convert_x(1, 1)
    unit_slot(0, 1, (1,))
    unit_first(1, (1,))
    pass_extra(last)
    mix_first(1)
    wait_sibling(2)
    convert_x(2, 1)
    unit_slot(0, 2, (1,))
    unit_first(2, (1,))
    mix_first(2)
    convert_x(3, 0)
    wait_sibling(3)
    convert_x(3, 1)
    unit_first(3)
    mix_first(3)
    send_far(first_part)
    wait_p(3, 0)
    wait_p(3, 1)
    convert_p(3)
    for b in range(3):
        unit_slot(3, b)
        mix_second(b)
    unit_part(second_part, z_second, 24, 3)
    mix_second(3)
    send_far(second_part)
    send_near(second_part)
    send_near(first_part)
    finish(second_part)
    finish(first_part)

    for copy in sent:
        copy.wait_send()

    @pl.when(full)
    def _():
        for copy in sent_full:
            copy.wait_send()


def filter_step(*operands):
    dma = pltpu.SemaphoreType.DMA
    vmem = pl.BlockSpec(memory_space=pltpu.VMEM)
    smem = pl.BlockSpec(memory_space=pltpu.SMEM)
    anywhere = pl.BlockSpec(memory_space=pl.ANY)
    return pl.pallas_call(
        kernel,
        out_shape=jax.ShapeDtypeStruct((8, 256, 128), F32),
        in_specs=[anywhere] * 2 + [vmem] * 4 + [smem] * 3,
        out_specs=vmem,
        scratch_shapes=[
            pltpu.VMEM((4, 2, 2, 2, 32, NB), F32),
            pltpu.VMEM((16, 2, 32, NB), BF16),
            pltpu.VMEM((16, 2, 32, NB), BF16),
            pltpu.VMEM((4, 8, NB, 128), F32),
            pltpu.VMEM((4, 2, NB, 512), BF16),
            pltpu.VMEM((4, 2, NB, 512), BF16),
            pltpu.VMEM((16, 8, 32, 128), F32),
            pltpu.VMEM((32, 8, 32, 128), F32),
            pltpu.VMEM((40, 128), F32),
            pltpu.VMEM((3, 40, 128), F32),
            pltpu.VMEM((8, 40, 128), F32),
            pltpu.VMEM((4, 320, 512), BF16),
            pltpu.VMEM((4, 320, 512), BF16),
            pltpu.VMEM((2, 8, 8, 32, 128), F32),
            pltpu.VMEM((2, 4, 8, 32, 128), F32),
            pltpu.VMEM((2, 2, 2, 8, 32, 128), F32),
            dma, dma((2,)), dma((3, 2)), dma((4, 2)),
            dma((2, 2, 2)), dma((2, 2)), dma((4, 2)), dma((4, 2, 2)), dma((4, 2, 2)), dma((4, 2, 2)),
            dma((3,)), dma((3,)), dma((3,)), dma((4,)), dma((2,)), dma((2,)),
            dma((2, 3)), dma((2, 4)), dma((2, 2)), dma((2, 2)),
        ],
        compiler_params=pltpu.CompilerParams(
            collective_id=0, has_side_effects=True, vmem_limit_bytes=60 * 2**20
        ),
        cost_estimate=pl.CostEstimate(flops=30_000_000_000, bytes_accessed=40_000_000, transcendentals=0),
        name="filter_step",
    )(*operands)


def body(
    columns, panels, coefficients, channel_cols, used_slots, lambda_low, lambda_high, energies, contour
):
    return filter_step(
        columns, panels, jnp.transpose(coefficients, (2, 0, 1)), channel_cols, lambda_low, lambda_high,
        used_slots, energies, contour,
    )


def solution(mesh):
    return jax.shard_map(
        body,
        mesh=mesh,
        in_specs=(
            P("chan", None, None),
            P("mult", None, "chan", None),
            P("chan", None, "mult"),
            P("chan", None),
            P("chan"),
            P("chan", None),
            P("chan", None),
            P("chan"),
            P(),
        ),
        out_specs=P("chan", "mult", None),
        check_vma=False,
    )
```
